512 devices in a mesh: rep: 4 (over z_lo), ctx: 128 (over y, x, z_hi, core).
Axes of the slice: x: 4, y: 8, z: 8 (z_hi: 2, z_lo: 4; z = z_hi * 4 + z_lo), core: 2. Of those that a mesh axis runs over, the one named last changes fastest.
Arguments:
- inputs: bfloat16 [4, 16384, 256], P('rep', 'ctx'), may hold values from -6 to 6
- out_grad: bfloat16 [4, 16384, 256], P('rep', 'ctx'), may hold values from -6 to 6
- out_gate: bfloat16 [4, 16384, 256], P('rep', 'ctx'), may hold values from -6 to 6
- filter_param: float32 [16384, 256], P('ctx'), may hold values from -6 to 6
- skip_gain: float32 [256], replicated, may hold values from -4 to 4
Outputs:
- input_grad: bfloat16 [4, 16384, 256], P('rep', 'ctx')
- filter_grad: float32 [16384, 256], P('ctx', 'rep')
The draws below stay inside these ranges and needn't reach their ends.
All inputs are finite; a program needn't handle non-finite values.
Results may differ from the reference program's by a relative error of at most 0.001.
Values sent between devices are 32-bit elements; how exact they have to be, the bound alone decides.
No kernel may reach another device: no remote copies, remote signals or barrier semaphores. Data moves between devices by JAX's collectives and lax.ppermute only.
A program may use at most 64 MiB of HBM per device.

```python
import math
import jax
import jax.numpy as jnp
from jax import lax

CHANNELS = 256
SEQ_LEN = 16384
SEQS = 4


def block_levels(own_key, extent, shards, least, high):
    gain, own = 1.0, jax.random.fold_in(own_key, 6)
    for dim, shards_of in shards:
        steps = jnp.exp(jax.random.uniform(jax.random.fold_in(own, dim), (shards_of,), jnp.float32, least / len(shards), high / len(shards)))
        gain = gain * jnp.repeat(steps, extent[dim] // shards_of).reshape([-1 if axis == dim else 1 for axis in range(len(extent))])
    return gain


def scatter_about(stream_key, shape, deviation, most, shards=(), dtype=jnp.bfloat16):
    gain = block_levels(stream_key, shape, shards, -0.22, 0.18) if shards else 1.0
    entries = jax.random.normal(stream_key, shape, jnp.float32) * deviation * gain
    return jnp.minimum(jnp.maximum(entries, -most), most).astype(dtype)


def setup_inputs(seed: int = 0) -> dict:
    seeds = jax.random.split(jax.random.key(seed), 6)
    inputs = scatter_about(seeds[0], (SEQS, SEQ_LEN, CHANNELS), 1.0, 6.0, ((0, 4), (1, 128)))
    out_grad = scatter_about(seeds[1], (SEQS, SEQ_LEN, CHANNELS), 1.0, 6.0, ((0, 4), (1, 128)))
    out_gate = scatter_about(seeds[2], (SEQS, SEQ_LEN, CHANNELS), 1.0, 6.0, ((0, 4), (1, 128)))
    filter_param = scatter_about(seeds[3], (SEQ_LEN, CHANNELS), 1.0, 6.0, ((0, 128),), jnp.float32)
    skip_gain = scatter_about(seeds[4], (CHANNELS,), 1.0, 4.0, (), jnp.float32)
    return {"inputs": inputs, "out_grad": out_grad, "out_gate": out_gate, "filter_param": filter_param, "skip_gain": skip_gain}


def reference(inputs, out_grad, out_gate, filter_param, skip_gain):
    padded = 2 * SEQ_LEN
    norm_scale = 1.0 / math.sqrt(SEQ_LEN)
    gated = out_grad.astype(jnp.float32) * out_gate.astype(jnp.float32)
    filt = filter_param * norm_scale
    gated_spec = jnp.fft.rfft(gated, n=padded, axis=1)
    input_spec = jnp.fft.rfft(inputs.astype(jnp.float32), n=padded, axis=1)
    filter_spec = jnp.fft.rfft(filt, n=padded, axis=0)
    conv_back = jnp.fft.irfft(gated_spec * jnp.conj(filter_spec)[None], n=padded, axis=1)[:, :SEQ_LEN]
    input_grad = (conv_back + skip_gain[None, None, :] * gated).astype(jnp.bfloat16)
    summed = lax.optimization_barrier(jnp.sum(gated_spec * jnp.conj(input_spec), axis=0))
    filter_grad = jnp.fft.irfft(summed, n=padded, axis=0)[:SEQ_LEN] * norm_scale
    return (input_grad, filter_grad)
```

```python
import math

import jax
import jax.numpy as jnp
import numpy as np
from jax import lax
from jax.experimental import pallas as pl
from jax.experimental.pallas import tpu as pltpu
from jax.sharding import PartitionSpec as P

highest = lax.Precision.HIGHEST


def tables(members, stride):
    padded = 2 * members * stride
    t1 = np.arange(members)
    t2 = np.arange(stride)
    odd = 2 * np.arange(members) + 1
    outer = 2.0 * np.pi / (4 * members) * (odd[:, None] * t1[None, :] % (4 * members))
    twist = 2.0 * np.pi / (2 * padded) * (odd[:, None] * t2[None, :] % (2 * padded))
    inner = 2.0 * np.pi / stride * (t2[:, None] * t2[None, :] % stride)
    first = np.concatenate([np.cos(outer), -np.sin(outer)], axis=0)
    second = np.block([[np.cos(inner), -np.sin(inner)], [np.sin(inner), np.cos(inner)]])
    scale = 2.0 / padded / math.sqrt(members * stride)
    return [
        np.asarray(table, np.float32)
        for table in (first, np.cos(twist), np.sin(twist), second, second.T, first.T * scale)
    ]


def pack_kernel(inputs_ref, grad_ref, gate_ref, filter_ref, out_ref):
    half = inputs_ref.shape[1] // 2
    gated = grad_ref[...].astype(jnp.float32) * gate_ref[...].astype(jnp.float32)
    signals = (gated, inputs_ref[...].astype(jnp.float32), filter_ref[...])
    for index, signal in enumerate(signals):
        for part in range(2):
            block = signal[:, part * half : (part + 1) * half]
            out_ref[pl.ds(2 * index + part, half, stride=6), :] = block.T


def spectra_kernel(
    signal_ref, first_ref, cos_ref, sin_ref, second_ref, back_ref, last_ref, out_ref
):
    stride = signal_ref.shape[1]
    members = signal_ref.shape[0] // 6
    signals = [signal_ref[pl.ds(row, members, stride=6), :] for row in range(6)]
    partial = jnp.dot(first_ref[...], jnp.concatenate(signals, axis=1), precision=highest)
    cosine = cos_ref[...]
    sine = sin_ref[...]
    turned = []
    for row in range(6):
        real = partial[:members, row * stride : (row + 1) * stride]
        imag = partial[members:, row * stride : (row + 1) * stride]
        turned.append(
            jnp.concatenate([real * cosine + imag * sine, imag * cosine - real * sine], axis=1)
        )
    spectrum = jnp.dot(jnp.concatenate(turned, axis=0), second_ref[...], precision=highest)
    parts = [spectrum[row * members : (row + 1) * members] for row in range(6)]
    products = []
    for one, other in ((0, 4), (1, 5), (0, 2), (1, 3)):
        real, imag = parts[one][:, :stride], parts[one][:, stride:]
        other_real, other_imag = parts[other][:, :stride], parts[other][:, stride:]
        products.append(
            jnp.concatenate(
                [real * other_real + imag * other_imag, imag * other_real - real * other_imag],
                axis=1,
            )
        )
    restored = jnp.dot(jnp.concatenate(products, axis=0), back_ref[...], precision=highest)
    columns = []
    for row in range(4):
        real = restored[row * members : (row + 1) * members, :stride]
        imag = restored[row * members : (row + 1) * members, stride:]
        columns.append(
            jnp.concatenate([real * cosine - imag * sine, imag * cosine + real * sine], axis=0)
        )
    values = jnp.dot(last_ref[...], jnp.concatenate(columns, axis=1), precision=highest)
    for row in range(4):
        out_ref[pl.ds(row, members, stride=4), :] = values[:, row * stride : (row + 1) * stride]


def pick_kernel(returned_ref, out_ref):
    members = returned_ref.shape[0] // 4
    for part in range(2):
        out_ref[part * members : (part + 1) * members, :] = returned_ref[
            pl.ds(2 + part, members, stride=4), :
        ]


def input_kernel(returned_ref, grad_ref, gate_ref, skip_ref, out_ref):
    members = returned_ref.shape[0] // 4
    gated = grad_ref[...].astype(jnp.float32) * gate_ref[...].astype(jnp.float32)
    skipped = gated * skip_ref[...]
    for part in range(2):
        columns = slice(part * members, (part + 1) * members)
        block = returned_ref[pl.ds(part, members, stride=4), :]
        out_ref[:, columns] = (block.T + skipped[:, columns]).astype(jnp.bfloat16)


def filter_kernel(pieces_ref, out_ref):
    count = out_ref.shape[1]
    total = pieces_ref[:count, :]
    for piece in range(1, pieces_ref.shape[0] // count):
        total = total + pieces_ref[piece * count : (piece + 1) * count, :]
    out_ref[...] = total.T


def local(inputs, out_grad, out_gate, filter_param, skip_gain):
    members = lax.axis_size("ctx")
    seqs = lax.axis_size("rep")
    stride, channels = filter_param.shape
    f32 = jnp.float32
    packed = pl.pallas_call(
        pack_kernel, out_shape=jax.ShapeDtypeStruct((members * 6, stride), f32)
    )(inputs[0], out_grad[0], out_gate[0], filter_param)
    spread = lax.all_to_all(packed, "ctx", split_axis=0, concat_axis=0, tiled=True)
    values = pl.pallas_call(
        spectra_kernel, out_shape=jax.ShapeDtypeStruct((members * 4, stride), f32)
    )(spread, *tables(members, stride))
    returned = lax.all_to_all(values, "ctx", split_axis=0, concat_axis=0, tiled=True)
    picked = pl.pallas_call(
        pick_kernel, out_shape=jax.ShapeDtypeStruct((channels, stride), f32)
    )(returned)
    pieces = lax.all_to_all(picked, "rep", split_axis=0, concat_axis=0, tiled=True)
    input_part = pl.pallas_call(
        input_kernel, out_shape=jax.ShapeDtypeStruct((stride, channels), jnp.bfloat16)
    )(returned, out_grad[0], out_gate[0], skip_gain[None, :])
    filter_part = pl.pallas_call(
        filter_kernel, out_shape=jax.ShapeDtypeStruct((stride, channels // seqs), f32)
    )(pieces)
    return (input_part[None], filter_part)


def solution(mesh):
    return jax.shard_map(
        local,
        mesh=mesh,
        in_specs=(
            P("rep", "ctx", None),
            P("rep", "ctx", None),
            P("rep", "ctx", None),
            P("ctx", None),
            P(),
        ),
        out_specs=(P("rep", "ctx", None), P("ctx", "rep")),
        check_vma=False,
    )
```

```python
import math

import jax
import jax.numpy as jnp
import numpy as np
from jax import lax
from jax.experimental import pallas as pl
from jax.experimental.pallas import tpu as pltpu
from jax.sharding import PartitionSpec as P


def halves(values):
    high = values.astype(jnp.bfloat16)
    return high, (values - high.astype(jnp.float32)).astype(jnp.bfloat16)


def product(left, right):
    def dot(one, other):
        return jnp.dot(one, other, preferred_element_type=jnp.float32)

    total = dot(left[0], right[0])
    if right[1] is not None:
        total = total + dot(left[0], right[1])
    return total + dot(left[1], right[0])


def tables(members, stride):
    padded = 2 * members * stride
    t1 = np.arange(members)
    t2 = np.arange(stride)
    odd = 2 * np.arange(members) + 1
    outer = 2.0 * np.pi / (4 * members) * (odd[:, None] * t1[None, :] % (4 * members))
    twist = 2.0 * np.pi / (2 * padded) * (odd[:, None] * t2[None, :] % (2 * padded))
    inner = 2.0 * np.pi / stride * (t2[:, None] * t2[None, :] % stride)
    first = np.concatenate([np.cos(outer), -np.sin(outer)], axis=0)
    second = np.block([[np.cos(inner), -np.sin(inner)], [np.sin(inner), np.cos(inner)]])
    scale = 2.0 / padded / math.sqrt(members * stride)
    result = [np.asarray(np.cos(twist), np.float32), np.asarray(np.sin(twist), np.float32)]
    for table in (first, second, second.T, first.T * scale):
        high = table.astype(jnp.bfloat16)
        result += [high, (table - high.astype(np.float64)).astype(jnp.bfloat16)]
    return result


def pack_kernel(inputs_ref, grad_ref, gate_ref, filter_ref, out_ref):
    half = inputs_ref.shape[1] // 2
    gated = grad_ref[...].astype(jnp.float32) * gate_ref[...].astype(jnp.float32)
    signals = (gated, inputs_ref[...].astype(jnp.float32), filter_ref[...])
    for index, signal in enumerate(signals):
        for part in range(2):
            block = signal[:, part * half : (part + 1) * half]
            out_ref[pl.ds(2 * index + part, half, stride=6), :] = block.T


def spectra_kernel(signal_ref, cos_ref, sin_ref, *refs):
    first, second, back, last = [(refs[at][...], refs[at + 1][...]) for at in (0, 2, 4, 6)]
    out_ref = refs[8]
    stride = signal_ref.shape[1]
    members = signal_ref.shape[0] // 6
    signals = [signal_ref[pl.ds(row, members, stride=6), :] for row in range(6)]
    cosine = cos_ref[...]
    sine = sin_ref[...]
    partial = []
    for row in range(0, 6, 2):
        pair = jnp.concatenate(signals[row : row + 2], axis=1)
        sides = (pair.astype(jnp.bfloat16), None) if row == 2 else halves(pair)
        both = product(first, sides)
        partial += [both[:, :stride], both[:, stride:]]
    turned = []
    for value in partial:
        real, imag = value[:members], value[members:]
        turned.append(
            jnp.concatenate([real * cosine + imag * sine, imag * cosine - real * sine], axis=1)
        )
    parts = [product(halves(value), second) for value in turned]
    columns = []
    for one, other in ((0, 4), (1, 5), (0, 2), (1, 3)):
        real, imag = parts[one][:, :stride], parts[one][:, stride:]
        other_real, other_imag = parts[other][:, :stride], parts[other][:, stride:]
        value = jnp.concatenate(
            [real * other_real + imag * other_imag, imag * other_real - real * other_imag], axis=1
        )
        restored = product(halves(value), back)
        real, imag = restored[:, :stride], restored[:, stride:]
        columns.append(
            jnp.concatenate([real * cosine - imag * sine, imag * cosine + real * sine], axis=0)
        )
    for row in range(0, 4, 2):
        values = product(last, halves(jnp.concatenate(columns[row : row + 2], axis=1)))
        for part in range(2):
            out_ref[pl.ds(row + part, members, stride=4), :] = values[
                :, part * stride : (part + 1) * stride
            ]


def pick_kernel(returned_ref, out_ref):
    members = returned_ref.shape[0] // 4
    for part in range(2):
        out_ref[part * members : (part + 1) * members, :] = returned_ref[
            pl.ds(2 + part, members, stride=4), :
        ]


def input_kernel(returned_ref, grad_ref, gate_ref, skip_ref, out_ref):
    members = returned_ref.shape[0] // 4
    gated = grad_ref[...].astype(jnp.float32) * gate_ref[...].astype(jnp.float32)
    skipped = gated * skip_ref[...]
    for part in range(2):
        columns = slice(part * members, (part + 1) * members)
        block = returned_ref[pl.ds(part, members, stride=4), :]
        out_ref[:, columns] = (block.T + skipped[:, columns]).astype(jnp.bfloat16)


def filter_kernel(pieces_ref, out_ref):
    count = out_ref.shape[0]
    total = pieces_ref[:count, :]
    for piece in range(1, pieces_ref.shape[0] // count):
        total = total + pieces_ref[piece * count : (piece + 1) * count, :]
    out_ref[...] = total


def exchange(values, axis):
    rows, columns = values.shape
    pairs = values.reshape(rows // 2, 2, columns)
    pairs = lax.all_to_all(pairs, axis, split_axis=0, concat_axis=0, tiled=True)
    return pairs.reshape(rows, columns)


def local(inputs, out_grad, out_gate, filter_param, skip_gain):
    members = lax.axis_size("ctx")
    seqs = lax.axis_size("rep")
    stride, channels = filter_param.shape
    f32 = jnp.float32
    packed = pl.pallas_call(
        pack_kernel, out_shape=jax.ShapeDtypeStruct((members * 6, stride), f32)
    )(inputs[0], out_grad[0], out_gate[0], filter_param)
    spread = exchange(packed, "ctx")
    values = pl.pallas_call(
        spectra_kernel, out_shape=jax.ShapeDtypeStruct((members * 4, stride), f32)
    )(spread, *tables(members, stride))
    returned = exchange(values, "ctx")
    picked = pl.pallas_call(
        pick_kernel, out_shape=jax.ShapeDtypeStruct((channels, stride), f32)
    )(returned)
    pieces = exchange(picked, "rep")
    input_part = pl.pallas_call(
        input_kernel, out_shape=jax.ShapeDtypeStruct((stride, channels), jnp.bfloat16)
    )(returned, out_grad[0], out_gate[0], skip_gain[None, :])
    filter_part = pl.pallas_call(
        filter_kernel, out_shape=jax.ShapeDtypeStruct((channels // seqs, stride), f32)
    )(pieces)
    return (input_part[None], filter_part.T)


def solution(mesh):
    return jax.shard_map(
        local,
        mesh=mesh,
        in_specs=(
            P("rep", "ctx", None),
            P("rep", "ctx", None),
            P("rep", "ctx", None),
            P("ctx", None),
            P(),
        ),
        out_specs=(P("rep", "ctx", None), P("ctx", "rep")),
        check_vma=False,
    )
```

```python
import math

import jax
import jax.numpy as jnp
import numpy as np
from jax import lax
from jax.experimental import pallas as pl
from jax.experimental.pallas import tpu as pltpu
from jax.sharding import PartitionSpec as P


def halves(values):
    high = values.astype(jnp.bfloat16)
    return high, (values - high.astype(jnp.float32)).astype(jnp.bfloat16)


def product(left, right):
    def dot(one, other):
        return jnp.dot(one, other, preferred_element_type=jnp.float32)

    total = dot(left[0], right[0])
    if right[1] is not None:
        total = total + dot(left[0], right[1])
    return total + dot(left[1], right[0])


def tables(members, stride):
    padded = 2 * members * stride
    t1 = np.arange(members)
    t2 = np.arange(stride)
    odd = 2 * np.arange(members) + 1
    outer = 2.0 * np.pi / (4 * members) * (odd[:, None] * t1[None, :] % (4 * members))
    twist = 2.0 * np.pi / (2 * padded) * (odd[:, None] * t2[None, :] % (2 * padded))
    inner = 2.0 * np.pi / stride * (t2[:, None] * t2[None, :] % stride)
    first = np.concatenate([np.cos(outer), -np.sin(outer)], axis=0)
    second = np.block([[np.cos(inner), -np.sin(inner)], [np.sin(inner), np.cos(inner)]])
    scale = 2.0 / padded / math.sqrt(members * stride)
    result = [np.asarray(np.cos(twist), np.float32), np.asarray(np.sin(twist), np.float32)]
    for table in (first, second, second.T, first.T * scale):
        high = table.astype(jnp.bfloat16)
        result += [high, (table - high.astype(np.float64)).astype(jnp.bfloat16)]
    return result


def pack_kernel(inputs_ref, grad_ref, gate_ref, filter_ref, out_ref):
    half = inputs_ref.shape[1] // 2
    gated = grad_ref[...].astype(jnp.float32) * gate_ref[...].astype(jnp.float32)
    signals = (gated, inputs_ref[...].astype(jnp.float32), filter_ref[...])
    for index, signal in enumerate(signals):
        for part in range(2):
            block = signal[:, part * half : (part + 1) * half]
            out_ref[pl.ds(2 * index + part, half, stride=6), :] = block.T


def spectra_kernel(signal_ref, cos_ref, sin_ref, *refs):
    first, second, back, last = [(refs[at][...], refs[at + 1][...]) for at in (0, 2, 4, 6)]
    out_ref = refs[8]
    stride = signal_ref.shape[1]
    members = signal_ref.shape[0] // 6
    signals = [signal_ref[pl.ds(row, members, stride=6), :] for row in range(6)]
    cosine = cos_ref[...]
    sine = sin_ref[...]
    partial = []
    for row in range(0, 6, 2):
        pair = jnp.concatenate(signals[row : row + 2], axis=1)
        sides = (pair.astype(jnp.bfloat16), None) if row == 2 else halves(pair)
        both = product(first, sides)
        partial += [both[:, :stride], both[:, stride:]]
    turned = []
    for value in partial:
        real, imag = value[:members], value[members:]
        turned.append(
            jnp.concatenate([real * cosine + imag * sine, imag * cosine - real * sine], axis=1)
        )
    parts = [product(halves(value), second) for value in turned]
    columns = []
    for one, other in ((0, 4), (1, 5), (0, 2), (1, 3)):
        real, imag = parts[one][:, :stride], parts[one][:, stride:]
        other_real, other_imag = parts[other][:, :stride], parts[other][:, stride:]
        value = jnp.concatenate(
            [real * other_real + imag * other_imag, imag * other_real - real * other_imag], axis=1
        )
        restored = product(halves(value), back)
        real, imag = restored[:, :stride], restored[:, stride:]
        columns.append(
            jnp.concatenate([real * cosine - imag * sine, imag * cosine + real * sine], axis=0)
        )
    for row in range(0, 4, 2):
        values = product(last, halves(jnp.concatenate(columns[row : row + 2], axis=1)))
        for part in range(2):
            out_ref[pl.ds(row + part, members, stride=4), :] = values[
                :, part * stride : (part + 1) * stride
            ]


def pick_kernel(returned_ref, out_ref):
    members = returned_ref.shape[0] // 4
    for part in range(2):
        out_ref[part * members : (part + 1) * members, :] = returned_ref[
            pl.ds(2 + part, members, stride=4), :
        ]


def input_kernel(returned_ref, grad_ref, gate_ref, skip_ref, out_ref):
    members = returned_ref.shape[0] // 4
    gated = grad_ref[...].astype(jnp.float32) * gate_ref[...].astype(jnp.float32)
    skipped = gated * skip_ref[...]
    for part in range(2):
        columns = slice(part * members, (part + 1) * members)
        block = returned_ref[pl.ds(part, members, stride=4), :]
        out_ref[:, columns] = (block.T + skipped[:, columns]).astype(jnp.bfloat16)


def filter_kernel(pieces_ref, out_ref):
    count = out_ref.shape[0]
    total = pieces_ref[:count, :]
    for piece in range(1, pieces_ref.shape[0] // count):
        total = total + pieces_ref[piece * count : (piece + 1) * count, :]
    out_ref[...] = total


def exchange(values, axis):
    rows, columns = values.shape
    pairs = values.reshape(rows // 2, 2, columns)
    pairs = lax.all_to_all(pairs, axis, split_axis=0, concat_axis=0, tiled=True)
    return pairs.reshape(rows, columns)


def local(inputs, out_grad, out_gate, filter_param, skip_gain):
    members = lax.axis_size("ctx")
    seqs = lax.axis_size("rep")
    stride, channels = filter_param.shape
    f32 = jnp.float32
    def near(values):
        return pltpu.with_memory_space_constraint(values, pltpu.VMEM)

    packed = pl.pallas_call(pack_kernel, out_shape=pltpu.VMEM((members * 6, stride), f32))(
        inputs[0], out_grad[0], out_gate[0], filter_param
    )
    spread = exchange(packed, "ctx")
    constants = [near(jnp.asarray(table)) for table in tables(members, stride)]
    values = pl.pallas_call(spectra_kernel, out_shape=pltpu.VMEM((members * 4, stride), f32))(
        near(spread), *constants
    )
    returned = near(exchange(values, "ctx"))
    picked = pl.pallas_call(pick_kernel, out_shape=pltpu.VMEM((channels, stride), f32))(returned)
    pieces = exchange(picked, "rep")
    input_part = pl.pallas_call(
        input_kernel, out_shape=jax.ShapeDtypeStruct((stride, channels), jnp.bfloat16)
    )(returned, near(out_grad[0]), near(out_gate[0]), near(skip_gain[None, :]))
    filter_part = pl.pallas_call(
        filter_kernel, out_shape=jax.ShapeDtypeStruct((channels // seqs, stride), f32)
    )(near(pieces))
    return (input_part[None], filter_part.T)


def solution(mesh):
    return jax.shard_map(
        local,
        mesh=mesh,
        in_specs=(
            P("rep", "ctx", None),
            P("rep", "ctx", None),
            P("rep", "ctx", None),
            P("ctx", None),
            P(),
        ),
        out_specs=(P("rep", "ctx", None), P("ctx", "rep")),
        check_vma=False,
    )
```

```python
import functools
import math

import jax
import jax.numpy as jnp
import numpy as np
from jax import lax
from jax.experimental import pallas as pl
from jax.experimental.pallas import tpu as pltpu
from jax.sharding import Mesh
from jax.sharding import PartitionSpec as P


def halves(values):
    high = values.astype(jnp.bfloat16)
    return high, (values - high.astype(jnp.float32)).astype(jnp.bfloat16)


def product(left, right):
    def dot(one, other):
        return jnp.dot(one, other, preferred_element_type=jnp.float32)

    total = dot(left[0], right[0])
    if right[1] is not None:
        total = total + dot(left[0], right[1])
    return total + dot(left[1], right[0])


def tables(members, stride):
    padded = 2 * members * stride
    t1 = np.arange(members)
    t2 = np.arange(stride)
    odd = 2 * np.arange(members) + 1
    outer = 2.0 * np.pi / (4 * members) * (odd[:, None] * t1[None, :] % (4 * members))
    twist = 2.0 * np.pi / (2 * padded) * (odd[:, None] * t2[None, :] % (2 * padded))
    inner = 2.0 * np.pi / stride * (t2[:, None] * t2[None, :] % stride)
    first = np.concatenate([np.cos(outer), -np.sin(outer)], axis=0)
    second = np.block([[np.cos(inner), -np.sin(inner)], [np.sin(inner), np.cos(inner)]])
    scale = 2.0 / padded / math.sqrt(members * stride)
    result = [np.asarray(np.cos(twist), np.float32), np.asarray(np.sin(twist), np.float32)]
    for table in (first, second, second.T, first.T * scale):
        high = table.astype(jnp.bfloat16)
        result += [high, (table - high.astype(np.float64)).astype(jnp.bfloat16)]
    return result


def pack_kernel(quarters, inputs_ref, grad_ref, gate_ref, filter_ref, out_ref):
    gated = grad_ref[...].astype(jnp.float32) * gate_ref[...].astype(jnp.float32)
    signals = (gated, inputs_ref[...].astype(jnp.float32), filter_ref[...])
    run = filter_ref.shape[1] // (4 * quarters)
    for index, signal in enumerate(signals):
        turned = signal.T
        for block in range(4 * quarters):
            quarter, core, part = block // 4, block // 2 % 2, block % 2
            row = 6 * (2 * run * quarter + core) + 2 * index + part
            out_ref[pl.ds(row, run, stride=12), :] = turned[block * run : (block + 1) * run]


def spectra_kernel(signal_ref, cos_ref, sin_ref, *refs):
    first, second, back, last = [(refs[at][...], refs[at + 1][...]) for at in (0, 2, 4, 6)]
    out_ref = refs[8]
    stride = signal_ref.shape[1]
    members = signal_ref.shape[0] // 6
    signals = [signal_ref[pl.ds(row, members, stride=6), :] for row in range(6)]
    cosine = cos_ref[...]
    sine = sin_ref[...]
    partial = []
    for row in range(0, 6, 2):
        pair = jnp.concatenate(signals[row : row + 2], axis=1)
        sides = (pair.astype(jnp.bfloat16), None) if row == 2 else halves(pair)
        both = product(first, sides)
        partial += [both[:, :stride], both[:, stride:]]
    turned = []
    for value in partial:
        real, imag = value[:members], value[members:]
        turned.append(
            jnp.concatenate([real * cosine + imag * sine, imag * cosine - real * sine], axis=1)
        )
    parts = [product(halves(value), second) for value in turned]
    columns = []
    for one, other in ((0, 4), (1, 5), (0, 2), (1, 3)):
        real, imag = parts[one][:, :stride], parts[one][:, stride:]
        other_real, other_imag = parts[other][:, :stride], parts[other][:, stride:]
        value = jnp.concatenate(
            [real * other_real + imag * other_imag, imag * other_real - real * other_imag], axis=1
        )
        restored = product(halves(value), back)
        real, imag = restored[:, :stride], restored[:, stride:]
        columns.append(
            jnp.concatenate([real * cosine - imag * sine, imag * cosine + real * sine], axis=0)
        )
    for row in range(0, 4, 2):
        values = product(last, halves(jnp.concatenate(columns[row : row + 2], axis=1)))
        for part in range(2):
            out_ref[pl.ds(row + part, members, stride=4), :] = values[
                :, part * stride : (part + 1) * stride
            ]


def pick_kernel(quarters, returned_ref, filter_ref, input_ref):
    own = lax.axis_index("core") == 0
    chips = returned_ref.shape[0] // 8
    run = chips // quarters
    for quarter in range(quarters):
        for core in range(2):
            for part in range(2):
                row = (4 * quarter + 2 * core + part) * run
                filter_ref[row : row + run, :] = returned_ref[
                    pl.ds(8 * run * quarter + 4 * core + 2 + part, run, stride=8), :
                ]
    for part in range(2):
        input_ref[part * chips : (part + 1) * chips, :] = jnp.where(
            own,
            returned_ref[pl.ds(4 + part, chips, stride=8), :],
            returned_ref[pl.ds(part, chips, stride=8), :],
        )


def input_kernel(quarters, returned_ref, other_ref, grad_ref, gate_ref, skip_ref, out_ref):
    own = lax.axis_index("core") == 0
    chips = returned_ref.shape[0] // 8
    run = chips // quarters
    mine = [
        jnp.where(
            own,
            returned_ref[pl.ds(part, chips, stride=8), :],
            returned_ref[pl.ds(4 + part, chips, stride=8), :],
        )
        for part in range(2)
    ]
    others = [other_ref[part * chips : (part + 1) * chips, :] for part in range(2)]
    first = [jnp.where(own, one, other) for one, other in zip(mine, others)]
    second = [jnp.where(own, other, one) for one, other in zip(mine, others)]
    rows = []
    for quarter in range(quarters):
        for values in first + second:
            rows.append(values[quarter * run : (quarter + 1) * run])
    gated = grad_ref[...].astype(jnp.float32) * gate_ref[...].astype(jnp.float32)
    total = jnp.concatenate(rows, axis=0).T + gated * skip_ref[...]
    out_ref[...] = total.astype(jnp.bfloat16)


def filter_kernel(pieces_ref, out_ref):
    count = out_ref.shape[0]
    total = pieces_ref[:count, :]
    for start in range(count, pieces_ref.shape[0], count):
        total = total + pieces_ref[start : start + count, :]
    out_ref[...] = total


def exchange(values, axis):
    rows, columns = values.shape
    members = lax.axis_size(axis)
    wide = values.reshape(members, 1, rows // members * columns)
    wide = lax.all_to_all(wide, axis, split_axis=0, concat_axis=0, tiled=True)
    return wide.reshape(rows, columns)


def near(values):
    return pltpu.with_memory_space_constraint(values, pltpu.VMEM)


def local(inputs, out_grad, out_gate, filter_param, skip_gain):
    members = lax.axis_size(("chip", "core"))
    quarters = lax.axis_size("rep")
    stride, channels = filter_param.shape
    f32 = jnp.float32
    packed = pl.pallas_call(
        functools.partial(pack_kernel, quarters), out_shape=pltpu.VMEM((members * 6, stride), f32)
    )(inputs[0], out_grad[0], out_gate[0], filter_param)
    spread = exchange(packed, ("chip", "core"))
    constants = [near(jnp.asarray(table)) for table in tables(members, stride)]
    values = pl.pallas_call(spectra_kernel, out_shape=pltpu.VMEM((members * 4, stride), f32))(
        near(spread), *constants
    )
    returned = near(exchange(values, "chip"))
    filter_picked, input_picked = pl.pallas_call(
        functools.partial(pick_kernel, quarters),
        out_shape=[pltpu.VMEM((channels, stride), f32), pltpu.VMEM((members, stride), f32)],
    )(returned)
    pieces = lax.all_to_all(
        filter_picked, ("rep", "core"), split_axis=0, concat_axis=0, tiled=True
    )
    other = lax.ppermute(input_picked, "core", [(0, 1), (1, 0)])
    input_part = pl.pallas_call(
        functools.partial(input_kernel, quarters),
        out_shape=jax.ShapeDtypeStruct((stride, channels), jnp.bfloat16),
    )(returned, near(other), near(out_grad[0]), near(out_gate[0]), near(skip_gain[None, :]))
    filter_part = pl.pallas_call(
        filter_kernel, out_shape=jax.ShapeDtypeStruct((channels // quarters, stride), f32)
    )(near(pieces))
    return (input_part[None], filter_part.T)


def solution(mesh):
    seqs, members = mesh.devices.shape
    cores = Mesh(mesh.devices.reshape(seqs, members // 2, 2), ("rep", "chip", "core"))
    ctx = ("chip", "core")
    return jax.shard_map(
        local,
        mesh=cores,
        in_specs=(
            P("rep", ctx, None),
            P("rep", ctx, None),
            P("rep", ctx, None),
            P(ctx, None),
            P(),
        ),
        out_specs=(P("rep", ctx, None), P(ctx, "rep")),
        check_vma=False,
    )
```

```python
import functools
import math

import jax
import jax.numpy as jnp
import numpy as np
from jax import lax
from jax.experimental import pallas as pl
from jax.experimental.pallas import tpu as pltpu
from jax.sharding import Mesh
from jax.sharding import PartitionSpec as P


def halves(values):
    high = values.astype(jnp.bfloat16)
    return high, (values - high.astype(jnp.float32)).astype(jnp.bfloat16)


def product(left, right):
    def dot(one, other):
        return jnp.dot(one, other, preferred_element_type=jnp.float32)

    total = dot(left[0], right[0])
    if right[1] is not None:
        total = total + dot(left[0], right[1])
    return total + dot(left[1], right[0])


def tables(members, stride):
    padded = 2 * members * stride
    t1 = np.arange(members)
    t2 = np.arange(stride)
    odd = 2 * np.arange(members) + 1
    outer = 2.0 * np.pi / (4 * members) * (odd[:, None] * t1[None, :] % (4 * members))
    twist = 2.0 * np.pi / (2 * padded) * (odd[:, None] * t2[None, :] % (2 * padded))
    inner = 2.0 * np.pi / stride * (t2[:, None] * t2[None, :] % stride)
    first = np.concatenate([np.cos(outer), -np.sin(outer)], axis=0)
    second = np.block([[np.cos(inner), -np.sin(inner)], [np.sin(inner), np.cos(inner)]])
    scale = 2.0 / padded / math.sqrt(members * stride)
    result = [np.asarray(np.cos(twist), np.float32), np.asarray(np.sin(twist), np.float32)]
    for table in (first, second, second.T, first.T * scale):
        high = table.astype(jnp.bfloat16)
        result += [high, (table - high.astype(np.float64)).astype(jnp.bfloat16)]
    return result


def signals_by_channel(inputs_ref, grad_ref, gate_ref, filter_ref):
    gated = grad_ref[...].astype(jnp.float32) * gate_ref[...].astype(jnp.float32)
    return [signal.T for signal in (gated, inputs_ref[...].astype(jnp.float32), filter_ref[...])]


def hand_kernel(quarters, inputs_ref, grad_ref, gate_ref, filter_ref, out_ref):
    first = lax.axis_index("core") == 0
    run = filter_ref.shape[1] // (4 * quarters)
    row = 0
    for turned in signals_by_channel(inputs_ref, grad_ref, gate_ref, filter_ref):
        for part in range(2):
            for quarter in range(quarters):
                start = (4 * quarter + part) * run
                out_ref[row : row + run, :] = jnp.where(
                    first,
                    turned[start + 2 * run : start + 3 * run],
                    turned[start : start + run],
                )
                row += run


def pack_kernel(quarters, inputs_ref, grad_ref, gate_ref, filter_ref, out_ref):
    core = lax.axis_index("core")
    run = filter_ref.shape[1] // (4 * quarters)
    signals = signals_by_channel(inputs_ref, grad_ref, gate_ref, filter_ref)
    for index, turned in enumerate(signals):
        for part in range(2):
            for quarter in range(quarters):
                start = (4 * quarter + part) * run
                row = 12 * run * quarter + 2 * index + part
                out_ref[pl.ds(row + 6 * core, run, stride=12), :] = jnp.where(
                    core == 0,
                    turned[start : start + run],
                    turned[start + 2 * run : start + 3 * run],
                )


def merge_kernel(handed_ref, packed_ref, out_ref):
    core = lax.axis_index("core")
    chips = handed_ref.shape[0] // 6
    for row in range(6):
        out_ref[pl.ds(row + 6 * (1 - core), chips, stride=12), :] = handed_ref[
            row * chips : (row + 1) * chips, :
        ]


def spectra_kernel(signal_ref, cos_ref, sin_ref, *refs):
    first, second, back, last = [(refs[at][...], refs[at + 1][...]) for at in (0, 2, 4, 6)]
    out_ref = refs[8]
    stride = signal_ref.shape[1]
    members = signal_ref.shape[0] // 6
    signals = [signal_ref[pl.ds(row, members, stride=6), :] for row in range(6)]
    cosine = cos_ref[...]
    sine = sin_ref[...]
    partial = []
    for row in range(0, 6, 2):
        pair = jnp.concatenate(signals[row : row + 2], axis=1)
        sides = (pair.astype(jnp.bfloat16), None) if row == 2 else halves(pair)
        both = product(first, sides)
        partial += [both[:, :stride], both[:, stride:]]
    turned = []
    for value in partial:
        real, imag = value[:members], value[members:]
        turned.append(
            jnp.concatenate([real * cosine + imag * sine, imag * cosine - real * sine], axis=1)
        )
    parts = [product(halves(value), second) for value in turned]
    columns = []
    for one, other in ((0, 4), (1, 5), (0, 2), (1, 3)):
        real, imag = parts[one][:, :stride], parts[one][:, stride:]
        other_real, other_imag = parts[other][:, :stride], parts[other][:, stride:]
        value = jnp.concatenate(
            [real * other_real + imag * other_imag, imag * other_real - real * other_imag], axis=1
        )
        restored = product(halves(value), back)
        real, imag = restored[:, :stride], restored[:, stride:]
        columns.append(
            jnp.concatenate([real * cosine - imag * sine, imag * cosine + real * sine], axis=0)
        )
    for row in range(0, 4, 2):
        values = product(last, halves(jnp.concatenate(columns[row : row + 2], axis=1)))
        for part in range(2):
            out_ref[pl.ds(row + part, members, stride=4), :] = values[
                :, part * stride : (part + 1) * stride
            ]


def pick_kernel(quarters, returned_ref, filter_ref, input_ref):
    own = lax.axis_index("core") == 0
    chips = returned_ref.shape[0] // 8
    run = chips // quarters
    for quarter in range(quarters):
        for core in range(2):
            for part in range(2):
                row = (4 * quarter + 2 * core + part) * run
                filter_ref[row : row + run, :] = returned_ref[
                    pl.ds(8 * run * quarter + 4 * core + 2 + part, run, stride=8), :
                ]
    for part in range(2):
        input_ref[part * chips : (part + 1) * chips, :] = jnp.where(
            own,
            returned_ref[pl.ds(4 + part, chips, stride=8), :],
            returned_ref[pl.ds(part, chips, stride=8), :],
        )


def input_kernel(quarters, returned_ref, other_ref, grad_ref, gate_ref, skip_ref, out_ref):
    own = lax.axis_index("core") == 0
    chips = returned_ref.shape[0] // 8
    run = chips // quarters
    mine = [
        jnp.where(
            own,
            returned_ref[pl.ds(part, chips, stride=8), :],
            returned_ref[pl.ds(4 + part, chips, stride=8), :],
        )
        for part in range(2)
    ]
    others = [other_ref[part * chips : (part + 1) * chips, :] for part in range(2)]
    first = [jnp.where(own, one, other) for one, other in zip(mine, others)]
    second = [jnp.where(own, other, one) for one, other in zip(mine, others)]
    rows = []
    for quarter in range(quarters):
        for values in first + second:
            rows.append(values[quarter * run : (quarter + 1) * run])
    gated = grad_ref[...].astype(jnp.float32) * gate_ref[...].astype(jnp.float32)
    total = jnp.concatenate(rows, axis=0).T + gated * skip_ref[...]
    out_ref[...] = total.astype(jnp.bfloat16)


def filter_kernel(pieces_ref, out_ref):
    count = out_ref.shape[0]
    total = pieces_ref[:count, :]
    for start in range(count, pieces_ref.shape[0], count):
        total = total + pieces_ref[start : start + count, :]
    out_ref[...] = total


def exchange(values, axis):
    rows, columns = values.shape
    members = lax.axis_size(axis)
    wide = values.reshape(members, 1, rows // members * columns)
    wide = lax.all_to_all(wide, axis, split_axis=0, concat_axis=0, tiled=True)
    return wide.reshape(rows, columns)


def near(values):
    return pltpu.with_memory_space_constraint(values, pltpu.VMEM)


def local(inputs, out_grad, out_gate, filter_param, skip_gain):
    members = lax.axis_size(("chip", "core"))
    quarters = lax.axis_size("rep")
    stride, channels = filter_param.shape
    f32 = jnp.float32
    sources = (inputs[0], out_grad[0], out_gate[0], filter_param)
    handed = pl.pallas_call(
        functools.partial(hand_kernel, quarters), out_shape=pltpu.VMEM((members * 3, stride), f32)
    )(*sources)
    handed = lax.ppermute(handed, "core", [(0, 1), (1, 0)])
    packed = pl.pallas_call(
        functools.partial(pack_kernel, quarters), out_shape=pltpu.VMEM((members * 6, stride), f32)
    )(*sources)
    merged = pl.pallas_call(
        merge_kernel,
        out_shape=pltpu.VMEM((members * 6, stride), f32),
        input_output_aliases={1: 0},
    )(near(handed), near(packed))
    spread = exchange(merged, "chip")
    constants = [near(jnp.asarray(table)) for table in tables(members, stride)]
    values = pl.pallas_call(spectra_kernel, out_shape=pltpu.VMEM((members * 4, stride), f32))(
        near(spread), *constants
    )
    returned = near(exchange(values, "chip"))
    filter_picked, input_picked = pl.pallas_call(
        functools.partial(pick_kernel, quarters),
        out_shape=[pltpu.VMEM((channels, stride), f32), pltpu.VMEM((members, stride), f32)],
    )(returned)
    pieces = lax.all_to_all(
        filter_picked, ("rep", "core"), split_axis=0, concat_axis=0, tiled=True
    )
    other = lax.ppermute(input_picked, "core", [(0, 1), (1, 0)])
    input_part = pl.pallas_call(
        functools.partial(input_kernel, quarters),
        out_shape=jax.ShapeDtypeStruct((stride, channels), jnp.bfloat16),
    )(returned, near(other), near(out_grad[0]), near(out_gate[0]), near(skip_gain[None, :]))
    filter_part = pl.pallas_call(
        filter_kernel, out_shape=jax.ShapeDtypeStruct((channels // quarters, stride), f32)
    )(near(pieces))
    return (input_part[None], filter_part.T)


def solution(mesh):
    seqs, members = mesh.devices.shape
    cores = Mesh(mesh.devices.reshape(seqs, members // 2, 2), ("rep", "chip", "core"))
    ctx = ("chip", "core")
    return jax.shard_map(
        local,
        mesh=cores,
        in_specs=(
            P("rep", ctx, None),
            P("rep", ctx, None),
            P("rep", ctx, None),
            P(ctx, None),
            P(),
        ),
        out_specs=(P("rep", ctx, None), P(ctx, "rep")),
        check_vma=False,
    )
```

```python
import functools
import math

import jax
import jax.numpy as jnp
import numpy as np
from jax import lax
from jax.experimental import pallas as pl
from jax.experimental.pallas import tpu as pltpu
from jax.sharding import Mesh
from jax.sharding import PartitionSpec as P


def halves(values):
    high = values.astype(jnp.bfloat16)
    return high, (values - high.astype(jnp.float32)).astype(jnp.bfloat16)


def product(left, right):
    def dot(one, other):
        return jnp.dot(one, other, preferred_element_type=jnp.float32)

    total = dot(left[0], right[0])
    if right[1] is not None:
        total = total + dot(left[0], right[1])
    return total + dot(left[1], right[0])


def tables(members, stride):
    padded = 2 * members * stride
    t1 = np.arange(members).reshape(members // 2, 2).T.reshape(-1)
    t2 = np.arange(stride)
    odd = 2 * np.arange(members) + 1
    outer = 2.0 * np.pi / (4 * members) * (odd[:, None] * t1[None, :] % (4 * members))
    twist = 2.0 * np.pi / (2 * padded) * (odd[:, None] * t2[None, :] % (2 * padded))
    inner = 2.0 * np.pi / stride * (t2[:, None] * t2[None, :] % stride)
    first = np.concatenate([np.cos(outer), -np.sin(outer)], axis=0)
    second = np.block([[np.cos(inner), -np.sin(inner)], [np.sin(inner), np.cos(inner)]])
    scale = 2.0 / padded / math.sqrt(members * stride)
    result = [np.asarray(np.cos(twist), np.float32), np.asarray(np.sin(twist), np.float32)]
    last = first[:, np.argsort(t1)].T * scale
    for table in (first, second, second.T, last):
        high = table.astype(jnp.bfloat16)
        result += [high, (table - high.astype(np.float64)).astype(jnp.bfloat16)]
    return result


def pack_kernel(quarters, inputs_ref, grad_ref, gate_ref, filter_ref, out_ref):
    gated = grad_ref[...].astype(jnp.float32) * gate_ref[...].astype(jnp.float32)
    signals = (gated, inputs_ref[...].astype(jnp.float32), filter_ref[...])
    run = filter_ref.shape[1] // (4 * quarters)
    for index, signal in enumerate(signals):
        turned = signal.T
        for block in range(4 * quarters):
            quarter, core, part = block // 4, block // 2 % 2, block % 2
            row = 6 * run * (quarters * core + quarter) + 2 * index + part
            out_ref[pl.ds(row, run, stride=6), :] = turned[block * run : (block + 1) * run]


def spectra_kernel(signal_ref, cos_ref, sin_ref, *refs):
    first, second, back, last = [(refs[at][...], refs[at + 1][...]) for at in (0, 2, 4, 6)]
    out_ref = refs[8]
    stride = signal_ref.shape[1]
    members = signal_ref.shape[0] // 6
    signals = [signal_ref[pl.ds(row, members, stride=6), :] for row in range(6)]
    cosine = cos_ref[...]
    sine = sin_ref[...]
    partial = []
    for row in range(0, 6, 2):
        pair = jnp.concatenate(signals[row : row + 2], axis=1)
        sides = (pair.astype(jnp.bfloat16), None) if row == 2 else halves(pair)
        both = product(first, sides)
        partial += [both[:, :stride], both[:, stride:]]
    turned = []
    for value in partial:
        real, imag = value[:members], value[members:]
        turned.append(
            jnp.concatenate([real * cosine + imag * sine, imag * cosine - real * sine], axis=1)
        )
    parts = [product(halves(value), second) for value in turned]
    columns = []
    for one, other in ((0, 4), (1, 5), (0, 2), (1, 3)):
        real, imag = parts[one][:, :stride], parts[one][:, stride:]
        other_real, other_imag = parts[other][:, :stride], parts[other][:, stride:]
        value = jnp.concatenate(
            [real * other_real + imag * other_imag, imag * other_real - real * other_imag], axis=1
        )
        restored = product(halves(value), back)
        real, imag = restored[:, :stride], restored[:, stride:]
        columns.append(
            jnp.concatenate([real * cosine - imag * sine, imag * cosine + real * sine], axis=0)
        )
    for row in range(0, 4, 2):
        values = product(last, halves(jnp.concatenate(columns[row : row + 2], axis=1)))
        for part in range(2):
            out_ref[pl.ds(row + part, members, stride=4), :] = values[
                :, part * stride : (part + 1) * stride
            ]


def pick_kernel(quarters, returned_ref, filter_ref, input_ref):
    own = lax.axis_index("core") == 0
    chips = returned_ref.shape[0] // 8
    run = chips // quarters
    for quarter in range(quarters):
        for core in range(2):
            for part in range(2):
                row = (4 * quarter + 2 * core + part) * run
                filter_ref[row : row + run, :] = returned_ref[
                    pl.ds(8 * run * quarter + 4 * core + 2 + part, run, stride=8), :
                ]
    for part in range(2):
        input_ref[part * chips : (part + 1) * chips, :] = jnp.where(
            own,
            returned_ref[pl.ds(4 + part, chips, stride=8), :],
            returned_ref[pl.ds(part, chips, stride=8), :],
        )


def input_kernel(quarters, returned_ref, other_ref, grad_ref, gate_ref, skip_ref, out_ref):
    own = lax.axis_index("core") == 0
    chips = returned_ref.shape[0] // 8
    run = chips // quarters
    mine = [
        jnp.where(
            own,
            returned_ref[pl.ds(part, chips, stride=8), :],
            returned_ref[pl.ds(4 + part, chips, stride=8), :],
        )
        for part in range(2)
    ]
    others = [other_ref[part * chips : (part + 1) * chips, :] for part in range(2)]
    first = [jnp.where(own, one, other) for one, other in zip(mine, others)]
    second = [jnp.where(own, other, one) for one, other in zip(mine, others)]
    rows = []
    for quarter in range(quarters):
        for values in first + second:
            rows.append(values[quarter * run : (quarter + 1) * run])
    gated = grad_ref[...].astype(jnp.float32) * gate_ref[...].astype(jnp.float32)
    total = jnp.concatenate(rows, axis=0).T + gated * skip_ref[...]
    out_ref[...] = total.astype(jnp.bfloat16)


def filter_kernel(pieces_ref, out_ref):
    count = out_ref.shape[0]
    total = pieces_ref[:count, :]
    for start in range(count, pieces_ref.shape[0], count):
        total = total + pieces_ref[start : start + count, :]
    out_ref[...] = total


def exchange(values, axis):
    rows, columns = values.shape
    members = lax.axis_size(axis)
    wide = values.reshape(members, 1, rows // members * columns)
    wide = lax.all_to_all(wide, axis, split_axis=0, concat_axis=0, tiled=True)
    return wide.reshape(rows, columns)


def near(values):
    return pltpu.with_memory_space_constraint(values, pltpu.VMEM)


def local(inputs, out_grad, out_gate, filter_param, skip_gain):
    members = lax.axis_size(("chip", "core"))
    quarters = lax.axis_size("rep")
    stride, channels = filter_param.shape
    f32 = jnp.float32
    packed = pl.pallas_call(
        functools.partial(pack_kernel, quarters), out_shape=pltpu.VMEM((members * 6, stride), f32)
    )(inputs[0], out_grad[0], out_gate[0], filter_param)
    spread = exchange(packed, ("core", "chip"))
    constants = [near(jnp.asarray(table)) for table in tables(members, stride)]
    values = pl.pallas_call(spectra_kernel, out_shape=pltpu.VMEM((members * 4, stride), f32))(
        near(spread), *constants
    )
    returned = near(exchange(values, "chip"))
    filter_picked, input_picked = pl.pallas_call(
        functools.partial(pick_kernel, quarters),
        out_shape=[pltpu.VMEM((channels, stride), f32), pltpu.VMEM((members, stride), f32)],
    )(returned)
    pieces = lax.all_to_all(
        filter_picked, ("rep", "core"), split_axis=0, concat_axis=0, tiled=True
    )
    other = lax.ppermute(input_picked, "core", [(0, 1), (1, 0)])
    input_part = pl.pallas_call(
        functools.partial(input_kernel, quarters),
        out_shape=jax.ShapeDtypeStruct((stride, channels), jnp.bfloat16),
    )(returned, near(other), near(out_grad[0]), near(out_gate[0]), near(skip_gain[None, :]))
    filter_part = pl.pallas_call(
        filter_kernel, out_shape=jax.ShapeDtypeStruct((channels // quarters, stride), f32)
    )(near(pieces))
    return (input_part[None], filter_part.T)


def solution(mesh):
    seqs, members = mesh.devices.shape
    cores = Mesh(mesh.devices.reshape(seqs, members // 2, 2), ("rep", "chip", "core"))
    ctx = ("chip", "core")
    return jax.shard_map(
        local,
        mesh=cores,
        in_specs=(
            P("rep", ctx, None),
            P("rep", ctx, None),
            P("rep", ctx, None),
            P(ctx, None),
            P(),
        ),
        out_specs=(P("rep", ctx, None), P(ctx, "rep")),
        check_vma=False,
    )
```

```python
import functools
import math

import jax
import jax.numpy as jnp
import numpy as np
from jax import lax
from jax.experimental import pallas as pl
from jax.experimental.pallas import tpu as pltpu
from jax.sharding import Mesh
from jax.sharding import PartitionSpec as P


def halves(values):
    high = values.astype(jnp.bfloat16)
    return high, (values - high.astype(jnp.float32)).astype(jnp.bfloat16)


def product(left, right):
    def dot(one, other):
        return jnp.dot(one, other, preferred_element_type=jnp.float32)

    total = dot(left[0], right[0])
    if right[1] is not None:
        total = total + dot(left[0], right[1])
    return total + dot(left[1], right[0])


def tables(members, stride):
    padded = 2 * members * stride
    t1 = np.arange(members)
    t2 = np.arange(stride)
    odd = 2 * np.arange(members) + 1
    outer = 2.0 * np.pi / (4 * members) * (odd[:, None] * t1[None, :] % (4 * members))
    twist = 2.0 * np.pi / (2 * padded) * (odd[:, None] * t2[None, :] % (2 * padded))
    inner = 2.0 * np.pi / stride * (t2[:, None] * t2[None, :] % stride)
    first = np.concatenate([np.cos(outer), -np.sin(outer)], axis=0)
    second = np.block([[np.cos(inner), -np.sin(inner)], [np.sin(inner), np.cos(inner)]])
    scale = 2.0 / padded / math.sqrt(members * stride)
    result = [np.asarray(np.cos(twist), np.float32), np.asarray(np.sin(twist), np.float32)]
    last = np.concatenate([first.T[0::2], first.T[1::2]], axis=0) * scale
    for table in (first, second, second.T, last):
        high = table.astype(jnp.bfloat16)
        result += [high, (table - high.astype(np.float64)).astype(jnp.bfloat16)]
    return result


def pack_kernel(inputs_ref, grad_ref, gate_ref, filter_ref, out_ref):
    gated = grad_ref[...].astype(jnp.float32) * gate_ref[...].astype(jnp.float32)
    signals = (gated, inputs_ref[...].astype(jnp.float32), filter_ref[...])
    chips = out_ref.shape[0] // 12
    for index, signal in enumerate(signals):
        turned = signal.T
        for quarter in range(4):
            row = 6 * (quarter // 2) + 2 * index + quarter % 2
            out_ref[pl.ds(row, chips, stride=12), :] = turned[
                quarter * chips : (quarter + 1) * chips
            ]


def spectra(signal_ref, first, second, cosine, sine):
    stride = signal_ref.shape[1]
    members = signal_ref.shape[0] // 6
    signals = [signal_ref[pl.ds(row, members, stride=6), :] for row in range(6)]
    partial = []
    for row in range(0, 6, 2):
        pair = jnp.concatenate(signals[row : row + 2], axis=1)
        sides = (pair.astype(jnp.bfloat16), None) if row == 2 else halves(pair)
        both = product(first, sides)
        partial += [both[:, :stride], both[:, stride:]]
    parts = []
    for value in partial:
        real, imag = value[:members], value[members:]
        turned = jnp.concatenate(
            [real * cosine + imag * sine, imag * cosine - real * sine], axis=1
        )
        parts.append(product(halves(turned), second))
    return parts


def correlated(one, other):
    stride = one.shape[1] // 2
    real, imag = one[:, :stride], one[:, stride:]
    other_real, other_imag = other[:, :stride], other[:, stride:]
    return jnp.concatenate(
        [real * other_real + imag * other_imag, imag * other_real - real * other_imag], axis=1
    )


def inverse(values, back, last, cosine, sine):
    columns = []
    for value in values:
        restored = product(halves(value), back)
        stride = restored.shape[1] // 2
        real, imag = restored[:, :stride], restored[:, stride:]
        columns.append(
            jnp.concatenate([real * cosine - imag * sine, imag * cosine + real * sine], axis=0)
        )
    return product(last, halves(jnp.concatenate(columns, axis=1)))


def pairs_of(refs):
    return [(refs[at][...], refs[at + 1][...]) for at in range(0, len(refs), 2)]


def filter_side_kernel(signal_ref, cos_ref, sin_ref, *refs):
    first, second, back, last = pairs_of(refs[:8])
    out_ref, product_ref = refs[8:]
    stride = signal_ref.shape[1]
    members = signal_ref.shape[0] // 6
    cosine, sine = cos_ref[...], sin_ref[...]
    parts = spectra(signal_ref, first, second, cosine, sine)
    values = inverse(
        [correlated(parts[0], parts[2]), correlated(parts[1], parts[3])], back, last, cosine, sine
    )
    for quarter in range(4):
        part = quarter % 2
        out_ref[quarter * members : (quarter + 1) * members, :] = values[
            :, part * stride : (part + 1) * stride
        ]
    for part in range(2):
        product_ref[part * members : (part + 1) * members, :] = correlated(
            parts[part], parts[4 + part]
        )


def input_side_kernel(product_ref, cos_ref, sin_ref, *refs):
    back, last = pairs_of(refs[:4])
    kept_ref, handed_ref = refs[4:]
    stride = cos_ref.shape[1]
    members = product_ref.shape[0] // 2
    chips = members // 2
    core = lax.axis_index("core")
    values = inverse(
        [product_ref[:members, :], product_ref[members:, :]],
        back,
        last,
        cos_ref[...],
        sin_ref[...],
    )
    for part in range(2):
        even = values[:chips, part * stride : (part + 1) * stride]
        odd = values[chips:, part * stride : (part + 1) * stride]
        rows = slice(part * chips, (part + 1) * chips)
        kept_ref[rows, :] = jnp.where(core == 0, even, odd)
        handed_ref[rows, :] = jnp.where(core == 0, odd, even)


def merge_kernel(kept_ref, handed_ref, pieces_ref, out_ref):
    first = lax.axis_index("core") == 0
    source = lax.axis_index("rep") // 2
    chips = out_ref.shape[0] // 5
    for part in range(2):
        mine = kept_ref[part * chips : (part + 1) * chips, :]
        other = handed_ref[part * chips : (part + 1) * chips, :]
        out_ref[pl.ds(part, chips, stride=5), :] = jnp.where(first, mine, other)
        out_ref[pl.ds(2 + part, chips, stride=5), :] = jnp.where(first, other, mine)
    total = None
    for member in range(4):
        start = pl.multiple_of((2 * member + source) * chips, chips)
        piece = pieces_ref[pl.ds(start, chips), :]
        total = piece if total is None else total + piece
    out_ref[pl.ds(4, chips, stride=5), :] = total


def last_kernel(returned_ref, grad_ref, gate_ref, skip_ref, input_ref, filter_ref):
    chips = returned_ref.shape[0] // 5
    filter_ref[...] = returned_ref[pl.ds(4, chips, stride=5), :]
    rows = [returned_ref[pl.ds(quarter, chips, stride=5), :] for quarter in range(4)]
    gated = grad_ref[...].astype(jnp.float32) * gate_ref[...].astype(jnp.float32)
    total = jnp.concatenate(rows, axis=0).T + gated * skip_ref[...]
    input_ref[...] = total.astype(jnp.bfloat16)


def exchange(values, axis):
    rows, columns = values.shape
    members = lax.axis_size(axis)
    wide = values.reshape(members, 1, rows // members * columns)
    wide = lax.all_to_all(wide, axis, split_axis=0, concat_axis=0, tiled=True)
    return wide.reshape(rows, columns)


def near(values):
    return pltpu.with_memory_space_constraint(values, pltpu.VMEM)


def local(inputs, out_grad, out_gate, filter_param, skip_gain):
    members = lax.axis_size(("chip", "core"))
    stride, channels = filter_param.shape
    f32 = jnp.float32
    packed = pl.pallas_call(pack_kernel, out_shape=pltpu.VMEM((members * 6, stride), f32))(
        inputs[0], out_grad[0], out_gate[0], filter_param
    )
    spread = exchange(packed, ("chip", "core"))
    constants = [near(jnp.asarray(table)) for table in tables(members, stride)]
    slots, products = pl.pallas_call(
        filter_side_kernel,
        out_shape=[
            pltpu.VMEM((members * 4, stride), f32),
            pltpu.VMEM((members * 2, 2 * stride), f32),
        ],
    )(near(spread), *constants)
    pieces = exchange(slots, ("rep", "core"))
    kept, handed = pl.pallas_call(
        input_side_kernel, out_shape=[pltpu.VMEM((members, stride), f32)] * 2
    )(near(products), *constants[:2], *constants[6:])
    handed = lax.ppermute(handed, "core", [(0, 1), (1, 0)])
    merged = pl.pallas_call(
        merge_kernel, out_shape=pltpu.VMEM((members // 2 * 5, stride), f32)
    )(near(kept), near(handed), near(pieces))
    returned = exchange(merged, "chip")
    input_part, filter_part = pl.pallas_call(
        last_kernel,
        out_shape=[
            jax.ShapeDtypeStruct((stride, channels), jnp.bfloat16),
            jax.ShapeDtypeStruct((channels // 4, stride), f32),
        ],
    )(near(returned), near(out_grad[0]), near(out_gate[0]), near(skip_gain[None, :]))
    return (input_part[None], filter_part.T)


def solution(mesh):
    seqs, members = mesh.devices.shape
    cores = Mesh(mesh.devices.reshape(seqs, members // 2, 2), ("rep", "chip", "core"))
    ctx = ("chip", "core")
    return jax.shard_map(
        local,
        mesh=cores,
        in_specs=(
            P("rep", ctx, None),
            P("rep", ctx, None),
            P("rep", ctx, None),
            P(ctx, None),
            P(),
        ),
        out_specs=(P("rep", ctx, None), P(ctx, "rep")),
        check_vma=False,
    )
```

```python
import functools
import math

import jax
import jax.numpy as jnp
import numpy as np
from jax import lax
from jax.experimental import pallas as pl
from jax.experimental.pallas import tpu as pltpu
from jax.sharding import Mesh
from jax.sharding import PartitionSpec as P


def halves(values):
    high = values.astype(jnp.bfloat16)
    return high, (values - high.astype(jnp.float32)).astype(jnp.bfloat16)


def product(left, right):
    def dot(one, other):
        return jnp.dot(one, other, preferred_element_type=jnp.float32)

    total = dot(left[0], right[0])
    if right[1] is not None:
        total = total + dot(left[0], right[1])
    return total + dot(left[1], right[0])


def tables(members, stride):
    padded = 2 * members * stride
    t1 = np.arange(members)
    t2 = np.arange(stride)
    odd = 2 * np.arange(members) + 1
    outer = 2.0 * np.pi / (4 * members) * (odd[:, None] * t1[None, :] % (4 * members))
    twist = 2.0 * np.pi / (2 * padded) * (odd[:, None] * t2[None, :] % (2 * padded))
    inner = 2.0 * np.pi / stride * (t2[:, None] * t2[None, :] % stride)
    first = np.concatenate([np.cos(outer), -np.sin(outer)], axis=0)
    second = np.block([[np.cos(inner), -np.sin(inner)], [np.sin(inner), np.cos(inner)]])
    scale = 2.0 / padded / math.sqrt(members * stride)
    result = [np.asarray(np.cos(twist), np.float32), np.asarray(np.sin(twist), np.float32)]
    last = np.concatenate([first.T[0::2], first.T[1::2]], axis=0) * scale
    for table in (first, second, second.T, last):
        high = table.astype(jnp.bfloat16)
        result += [high, (table - high.astype(np.float64)).astype(jnp.bfloat16)]
    return result


def pack_kernel(inputs_ref, grad_ref, gate_ref, filter_ref, skip_ref, out_ref, skipped_ref):
    gated = grad_ref[...].astype(jnp.float32) * gate_ref[...].astype(jnp.float32)
    skipped_ref[...] = gated * skip_ref[...]
    signals = (gated, inputs_ref[...].astype(jnp.float32), filter_ref[...])
    chips = out_ref.shape[0] // 12
    for index, signal in enumerate(signals):
        turned = signal.T
        for quarter in range(4):
            row = 6 * (quarter // 2) + 2 * index + quarter % 2
            out_ref[pl.ds(row, chips, stride=12), :] = turned[
                quarter * chips : (quarter + 1) * chips
            ]


def spectra(signal_ref, first, second, cosine, sine):
    stride = signal_ref.shape[1]
    members = signal_ref.shape[0] // 6
    signals = [signal_ref[pl.ds(row, members, stride=6), :] for row in range(6)]
    partial = []
    for row in range(0, 6, 2):
        pair = jnp.concatenate(signals[row : row + 2], axis=1)
        sides = (pair.astype(jnp.bfloat16), None) if row == 2 else halves(pair)
        both = product(first, sides)
        partial += [both[:, :stride], both[:, stride:]]
    parts = []
    for value in partial:
        real, imag = value[:members], value[members:]
        turned = jnp.concatenate(
            [real * cosine + imag * sine, imag * cosine - real * sine], axis=1
        )
        parts.append(product(halves(turned), second))
    return parts


def correlated(one, other):
    stride = one.shape[1] // 2
    real, imag = one[:, :stride], one[:, stride:]
    other_real, other_imag = other[:, :stride], other[:, stride:]
    return jnp.concatenate(
        [real * other_real + imag * other_imag, imag * other_real - real * other_imag], axis=1
    )


def inverse(values, back, last, cosine, sine):
    columns = []
    for value in values:
        restored = product(halves(value), back)
        stride = restored.shape[1] // 2
        real, imag = restored[:, :stride], restored[:, stride:]
        columns.append(
            jnp.concatenate([real * cosine - imag * sine, imag * cosine + real * sine], axis=0)
        )
    return product(last, halves(jnp.concatenate(columns, axis=1)))


def pairs_of(refs):
    return [(refs[at][...], refs[at + 1][...]) for at in range(0, len(refs), 2)]


def spectra_kernel(signal_ref, cos_ref, sin_ref, *refs):
    first, second, back, last = pairs_of(refs[:8])
    kept_ref, handed_ref = refs[8:]
    stride = signal_ref.shape[1]
    chips = signal_ref.shape[0] // 12
    even_core = lax.axis_index("core") == 0
    cosine, sine = cos_ref[...], sin_ref[...]
    parts = spectra(signal_ref, first, second, cosine, sine)
    for index, other in enumerate((2, 4)):
        products = [correlated(parts[part], parts[other + part]) for part in range(2)]
        values = inverse(products, back, last, cosine, sine)
        for part in range(2):
            even = values[:chips, part * stride : (part + 1) * stride]
            odd = values[chips:, part * stride : (part + 1) * stride]
            rows = slice((2 * index + part) * chips, (2 * index + part + 1) * chips)
            kept_ref[rows, :] = jnp.where(even_core, even, odd)
            handed_ref[rows, :] = jnp.where(even_core, odd, even)


def by_quarter(kept_ref, handed_ref, row, chips):
    even_core = lax.axis_index("core") == 0
    first, second = [], []
    for part in range(2):
        rows = slice(row + part * chips, row + (part + 1) * chips)
        mine, other = kept_ref[rows, :], handed_ref[rows, :]
        first.append(jnp.where(even_core, mine, other))
        second.append(jnp.where(even_core, other, mine))
    return first + second


def slots_kernel(kept_ref, handed_ref, out_ref):
    chips = out_ref.shape[0] // 4
    for quarter, block in enumerate(by_quarter(kept_ref, handed_ref, 0, chips)):
        out_ref[quarter * chips : (quarter + 1) * chips, :] = block


def merge_kernel(kept_ref, handed_ref, pieces_ref, out_ref):
    chips = out_ref.shape[0] // 5
    for quarter, block in enumerate(by_quarter(kept_ref, handed_ref, 2 * chips, chips)):
        out_ref[pl.ds(quarter, chips, stride=5), :] = block
    total = pieces_ref[:chips, :]
    for member in range(1, 4):
        total = total + pieces_ref[member * chips : (member + 1) * chips, :]
    out_ref[pl.ds(4, chips, stride=5), :] = total


def last_kernel(returned_ref, skipped_ref, input_ref, filter_ref):
    chips = returned_ref.shape[0] // 5
    filter_ref[...] = returned_ref[pl.ds(4, chips, stride=5), :]
    rows = [returned_ref[pl.ds(quarter, chips, stride=5), :] for quarter in range(4)]
    total = jnp.concatenate(rows, axis=0).T + skipped_ref[...]
    input_ref[...] = total.astype(jnp.bfloat16)


def exchange(values, axis):
    rows, columns = values.shape
    members = lax.axis_size(axis)
    wide = values.reshape(members, 1, rows // members * columns)
    wide = lax.all_to_all(wide, axis, split_axis=0, concat_axis=0, tiled=True)
    return wide.reshape(rows, columns)


def near(values):
    return pltpu.with_memory_space_constraint(values, pltpu.VMEM)


def local(inputs, out_grad, out_gate, filter_param, skip_gain):
    members = lax.axis_size(("chip", "core"))
    stride, channels = filter_param.shape
    f32 = jnp.float32
    packed, skipped = pl.pallas_call(
        pack_kernel,
        out_shape=[pltpu.VMEM((members * 6, stride), f32), pltpu.VMEM((stride, channels), f32)],
    )(inputs[0], out_grad[0], out_gate[0], filter_param, skip_gain[None, :])
    spread = exchange(packed, ("chip", "core"))
    constants = [near(jnp.asarray(table)) for table in tables(members, stride)]
    kept, handed = pl.pallas_call(
        spectra_kernel, out_shape=[pltpu.VMEM((members * 2, stride), f32)] * 2
    )(near(spread), *constants)
    handed = near(lax.ppermute(handed, "core", [(0, 1), (1, 0)]))
    kept = near(kept)
    slots = pl.pallas_call(slots_kernel, out_shape=pltpu.VMEM((members * 2, stride), f32))(
        kept, handed
    )
    pieces = exchange(slots, "rep")
    merged = pl.pallas_call(
        merge_kernel, out_shape=pltpu.VMEM((members // 2 * 5, stride), f32)
    )(kept, handed, near(pieces))
    returned = exchange(merged, "chip")
    input_part, filter_part = pl.pallas_call(
        last_kernel,
        out_shape=[
            jax.ShapeDtypeStruct((stride, channels), jnp.bfloat16),
            jax.ShapeDtypeStruct((channels // 4, stride), f32),
        ],
    )(near(returned), near(skipped))
    return (input_part[None], filter_part.T)


def solution(mesh):
    seqs, members = mesh.devices.shape
    cores = Mesh(mesh.devices.reshape(seqs, members // 2, 2), ("rep", "chip", "core"))
    ctx = ("chip", "core")
    return jax.shard_map(
        local,
        mesh=cores,
        in_specs=(
            P("rep", ctx, None),
            P("rep", ctx, None),
            P("rep", ctx, None),
            P(ctx, None),
            P(),
        ),
        out_specs=(P("rep", ctx, None), P(ctx, "rep")),
        check_vma=False,
    )
```

```python
import functools
import math

import jax
import jax.numpy as jnp
import numpy as np
from jax import lax
from jax.experimental import pallas as pl
from jax.experimental.pallas import tpu as pltpu
from jax.sharding import Mesh
from jax.sharding import PartitionSpec as P


def halves(values):
    high = values.astype(jnp.bfloat16)
    return high, (values - high.astype(jnp.float32)).astype(jnp.bfloat16)


def product(left, right):
    def dot(one, other):
        return jnp.dot(one, other, preferred_element_type=jnp.float32)

    total = dot(left[0], right[0])
    if right[1] is not None:
        total = total + dot(left[0], right[1])
    return total + dot(left[1], right[0])


def tables(members, stride):
    padded = 2 * members * stride
    t1 = np.arange(members).reshape(members // 2, 2).T.reshape(-1)
    t2 = np.arange(stride)
    odd = 2 * np.arange(members) + 1
    outer = 2.0 * np.pi / (4 * members) * (odd[:, None] * t1[None, :] % (4 * members))
    twist = 2.0 * np.pi / (2 * padded) * (odd[:, None] * t2[None, :] % (2 * padded))
    inner = 2.0 * np.pi / stride * (t2[:, None] * t2[None, :] % stride)
    first = np.concatenate([np.cos(outer), -np.sin(outer)], axis=0)
    second = np.block([[np.cos(inner), -np.sin(inner)], [np.sin(inner), np.cos(inner)]])
    scale = 2.0 / padded / math.sqrt(members * stride)
    result = [np.asarray(np.cos(twist), np.float32), np.asarray(np.sin(twist), np.float32)]
    for table in (first, second, second.T, first.T * scale):
        high = table.astype(jnp.bfloat16)
        result += [high, (table - high.astype(np.float64)).astype(jnp.bfloat16)]
    return result


def pack_kernel(inputs_ref, grad_ref, gate_ref, filter_ref, skip_ref, out_ref, skipped_ref):
    gated = grad_ref[...].astype(jnp.float32) * gate_ref[...].astype(jnp.float32)
    skipped_ref[...] = gated * skip_ref[...]
    signals = (gated, inputs_ref[...].astype(jnp.float32), filter_ref[...])
    chips = out_ref.shape[0] // 12
    for index, signal in enumerate(signals):
        turned = signal.T
        for quarter in range(4):
            row = 6 * chips * (quarter // 2) + 2 * index + quarter % 2
            out_ref[pl.ds(row, chips, stride=6), :] = turned[
                quarter * chips : (quarter + 1) * chips
            ]


def spectra(signal_ref, first, second, cosine, sine):
    stride = signal_ref.shape[1]
    members = signal_ref.shape[0] // 6
    signals = [signal_ref[pl.ds(row, members, stride=6), :] for row in range(6)]
    partial = []
    for row in range(0, 6, 2):
        pair = jnp.concatenate(signals[row : row + 2], axis=1)
        sides = (pair.astype(jnp.bfloat16), None) if row == 2 else halves(pair)
        both = product(first, sides)
        partial += [both[:, :stride], both[:, stride:]]
    parts = []
    for value in partial:
        real, imag = value[:members], value[members:]
        turned = jnp.concatenate(
            [real * cosine + imag * sine, imag * cosine - real * sine], axis=1
        )
        parts.append(product(halves(turned), second))
    return parts


def correlated(one, other):
    stride = one.shape[1] // 2
    real, imag = one[:, :stride], one[:, stride:]
    other_real, other_imag = other[:, :stride], other[:, stride:]
    return jnp.concatenate(
        [real * other_real + imag * other_imag, imag * other_real - real * other_imag], axis=1
    )


def inverse(values, back, last, cosine, sine):
    columns = []
    for value in values:
        restored = product(halves(value), back)
        stride = restored.shape[1] // 2
        real, imag = restored[:, :stride], restored[:, stride:]
        columns.append(
            jnp.concatenate([real * cosine - imag * sine, imag * cosine + real * sine], axis=0)
        )
    return product(last, halves(jnp.concatenate(columns, axis=1)))


def pairs_of(refs):
    return [(refs[at][...], refs[at + 1][...]) for at in range(0, len(refs), 2)]


def spectra_kernel(signal_ref, cos_ref, sin_ref, *refs):
    first, second, back, last = pairs_of(refs[:8])
    kept_ref, handed_ref = refs[8:]
    stride = signal_ref.shape[1]
    chips = signal_ref.shape[0] // 12
    even_core = lax.axis_index("core") == 0
    cosine, sine = cos_ref[...], sin_ref[...]
    parts = spectra(signal_ref, first, second, cosine, sine)
    for index, other in enumerate((2, 4)):
        products = [correlated(parts[part], parts[other + part]) for part in range(2)]
        values = inverse(products, back, last, cosine, sine)
        for part in range(2):
            even = values[:chips, part * stride : (part + 1) * stride]
            odd = values[chips:, part * stride : (part + 1) * stride]
            rows = slice((2 * index + part) * chips, (2 * index + part + 1) * chips)
            kept_ref[rows, :] = jnp.where(even_core, even, odd)
            handed_ref[rows, :] = jnp.where(even_core, odd, even)


def by_quarter(kept_ref, handed_ref, row, chips):
    even_core = lax.axis_index("core") == 0
    first, second = [], []
    for part in range(2):
        rows = slice(row + part * chips, row + (part + 1) * chips)
        mine, other = kept_ref[rows, :], handed_ref[rows, :]
        first.append(jnp.where(even_core, mine, other))
        second.append(jnp.where(even_core, other, mine))
    return first + second


def slots_kernel(kept_ref, handed_ref, out_ref):
    chips = out_ref.shape[0] // 4
    for quarter, block in enumerate(by_quarter(kept_ref, handed_ref, 0, chips)):
        out_ref[quarter * chips : (quarter + 1) * chips, :] = block


def merge_kernel(kept_ref, handed_ref, pieces_ref, out_ref):
    chips = out_ref.shape[0] // 5
    for quarter, block in enumerate(by_quarter(kept_ref, handed_ref, 2 * chips, chips)):
        out_ref[pl.ds(quarter, chips, stride=5), :] = block
    total = pieces_ref[:chips, :]
    for member in range(1, 4):
        total = total + pieces_ref[member * chips : (member + 1) * chips, :]
    out_ref[pl.ds(4, chips, stride=5), :] = total


def last_kernel(returned_ref, skipped_ref, input_ref, filter_ref):
    chips = returned_ref.shape[0] // 5
    filter_ref[...] = returned_ref[pl.ds(4, chips, stride=5), :]
    rows = [returned_ref[pl.ds(quarter, chips, stride=5), :] for quarter in range(4)]
    total = jnp.concatenate(rows, axis=0).T + skipped_ref[...]
    input_ref[...] = total.astype(jnp.bfloat16)


def exchange(values, axis):
    rows, columns = values.shape
    members = lax.axis_size(axis)
    wide = values.reshape(members, 1, rows // members * columns)
    wide = lax.all_to_all(wide, axis, split_axis=0, concat_axis=0, tiled=True)
    return wide.reshape(rows, columns)


def near(values):
    return pltpu.with_memory_space_constraint(values, pltpu.VMEM)


def local(inputs, out_grad, out_gate, filter_param, skip_gain):
    members = lax.axis_size(("chip", "core"))
    stride, channels = filter_param.shape
    f32 = jnp.float32
    packed, skipped = pl.pallas_call(
        pack_kernel,
        out_shape=[pltpu.VMEM((members * 6, stride), f32), pltpu.VMEM((stride, channels), f32)],
    )(inputs[0], out_grad[0], out_gate[0], filter_param, skip_gain[None, :])
    spread = exchange(packed, ("core", "chip"))
    constants = [near(jnp.asarray(table)) for table in tables(members, stride)]
    kept, handed = pl.pallas_call(
        spectra_kernel, out_shape=[pltpu.VMEM((members * 2, stride), f32)] * 2
    )(near(spread), *constants)
    handed = near(lax.ppermute(handed, "core", [(0, 1), (1, 0)]))
    kept = near(kept)
    slots = pl.pallas_call(slots_kernel, out_shape=pltpu.VMEM((members * 2, stride), f32))(
        kept, handed
    )
    pieces = exchange(slots, "rep")
    merged = pl.pallas_call(
        merge_kernel, out_shape=pltpu.VMEM((members // 2 * 5, stride), f32)
    )(kept, handed, near(pieces))
    returned = exchange(merged, "chip")
    input_part, filter_part = pl.pallas_call(
        last_kernel,
        out_shape=[
            jax.ShapeDtypeStruct((stride, channels), jnp.bfloat16),
            jax.ShapeDtypeStruct((channels // 4, stride), f32),
        ],
    )(near(returned), near(skipped))
    return (input_part[None], filter_part.T)


def solution(mesh):
    seqs, members = mesh.devices.shape
    cores = Mesh(mesh.devices.reshape(seqs, members // 2, 2), ("rep", "chip", "core"))
    ctx = ("chip", "core")
    return jax.shard_map(
        local,
        mesh=cores,
        in_specs=(
            P("rep", ctx, None),
            P("rep", ctx, None),
            P("rep", ctx, None),
            P(ctx, None),
            P(),
        ),
        out_specs=(P("rep", ctx, None), P(ctx, "rep")),
        check_vma=False,
    )
```

```python
import functools
import math

import jax
import jax.numpy as jnp
import numpy as np
from jax import lax
from jax.experimental import pallas as pl
from jax.experimental.pallas import tpu as pltpu
from jax.sharding import Mesh
from jax.sharding import PartitionSpec as P


def halves(values):
    high = values.astype(jnp.bfloat16)
    return high, (values - high.astype(jnp.float32)).astype(jnp.bfloat16)


def dot(left, right):
    return jnp.dot(left, right, preferred_element_type=jnp.float32)


def values_by_table(values, table):
    rows = values.shape[0]
    high, low = halves(values)
    both = dot(jnp.concatenate([high, low], axis=0), table[0])
    return both[:rows] + both[rows:] + dot(high, table[1])


def table_by_values(table, high, low):
    rows = table[0].shape[0]
    both = dot(jnp.concatenate(table, axis=0), high)
    total = both[:rows] + both[rows:]
    return total if low is None else total + dot(table[0], low)


def tables(members, stride):
    padded = 2 * members * stride
    t1 = np.arange(members)
    t2 = np.arange(stride)
    odd = 2 * np.arange(members) + 1
    outer = 2.0 * np.pi / (4 * members) * (odd[:, None] * t1[None, :] % (4 * members))
    twist = 2.0 * np.pi / (2 * padded) * (odd[:, None] * t2[None, :] % (2 * padded))
    inner = 2.0 * np.pi / stride * (t2[:, None] * t2[None, :] % stride)
    first = np.concatenate([np.cos(outer), -np.sin(outer)], axis=0)
    second = np.block([[np.cos(inner), -np.sin(inner)], [np.sin(inner), np.cos(inner)]])
    scale = 2.0 / padded / math.sqrt(members * stride)
    result = [np.asarray(np.cos(twist), np.float32), np.asarray(np.sin(twist), np.float32)]
    last = np.concatenate([first.T[0::2], first.T[1::2]], axis=0) * scale
    for table in (first, second, second.T, last):
        high = table.astype(jnp.bfloat16)
        result += [high, (table - high.astype(np.float64)).astype(jnp.bfloat16)]
    return result


def pack_kernel(inputs_ref, grad_ref, gate_ref, filter_ref, skip_ref, out_ref, skipped_ref):
    gated = grad_ref[...].astype(jnp.float32) * gate_ref[...].astype(jnp.float32)
    skipped_ref[...] = gated * skip_ref[...]
    signals = (gated, inputs_ref[...].astype(jnp.float32), filter_ref[...])
    chips = out_ref.shape[0] // 12
    for index, signal in enumerate(signals):
        turned = signal.T
        for quarter in range(4):
            row = 6 * (quarter // 2) + 2 * index + quarter % 2
            out_ref[pl.ds(row, chips, stride=12), :] = turned[
                quarter * chips : (quarter + 1) * chips
            ]


def spectra(signal_ref, first, second, cosine, sine):
    stride = signal_ref.shape[1]
    members = signal_ref.shape[0] // 6
    signals = [signal_ref[pl.ds(row, members, stride=6), :] for row in range(6)]
    parts = []
    for row in range(0, 6, 2):
        pair = jnp.concatenate(signals[row : row + 2], axis=1)
        sides = (pair.astype(jnp.bfloat16), None) if row == 2 else halves(pair)
        both = table_by_values(first, *sides)
        turned = []
        for value in (both[:, :stride], both[:, stride:]):
            real, imag = value[:members], value[members:]
            turned.append(
                jnp.concatenate([real * cosine + imag * sine, imag * cosine - real * sine], axis=1)
            )
        spectrum = values_by_table(jnp.concatenate(turned, axis=0), second)
        parts += [spectrum[:members], spectrum[members:]]
    return parts


def correlated(one, other):
    stride = one.shape[1] // 2
    real, imag = one[:, :stride], one[:, stride:]
    other_real, other_imag = other[:, :stride], other[:, stride:]
    return jnp.concatenate(
        [real * other_real + imag * other_imag, imag * other_real - real * other_imag], axis=1
    )


def inverse(values, back, last, cosine, sine):
    members, stride = cosine.shape
    restored = values_by_table(jnp.concatenate(values, axis=0), back)
    columns = []
    for start in (0, members):
        real = restored[start : start + members, :stride]
        imag = restored[start : start + members, stride:]
        columns.append(
            jnp.concatenate([real * cosine - imag * sine, imag * cosine + real * sine], axis=0)
        )
    return table_by_values(last, *halves(jnp.concatenate(columns, axis=1)))


def pairs_of(refs):
    return [(refs[at][...], refs[at + 1][...]) for at in range(0, len(refs), 2)]


def spectra_kernel(signal_ref, cos_ref, sin_ref, *refs):
    first, second, back, last = pairs_of(refs[:8])
    kept_ref, handed_ref = refs[8:]
    stride = signal_ref.shape[1]
    chips = signal_ref.shape[0] // 12
    even_core = lax.axis_index("core") == 0
    cosine, sine = cos_ref[...], sin_ref[...]
    parts = spectra(signal_ref, first, second, cosine, sine)
    for index, other in enumerate((2, 4)):
        products = [correlated(parts[part], parts[other + part]) for part in range(2)]
        values = inverse(products, back, last, cosine, sine)
        for part in range(2):
            even = values[:chips, part * stride : (part + 1) * stride]
            odd = values[chips:, part * stride : (part + 1) * stride]
            rows = slice((2 * index + part) * chips, (2 * index + part + 1) * chips)
            kept_ref[rows, :] = jnp.where(even_core, even, odd)
            handed_ref[rows, :] = jnp.where(even_core, odd, even)


def by_quarter(kept_ref, handed_ref, row, chips):
    even_core = lax.axis_index("core") == 0
    first, second = [], []
    for part in range(2):
        rows = slice(row + part * chips, row + (part + 1) * chips)
        mine, other = kept_ref[rows, :], handed_ref[rows, :]
        first.append(jnp.where(even_core, mine, other))
        second.append(jnp.where(even_core, other, mine))
    return first + second


def slots_kernel(kept_ref, handed_ref, out_ref):
    chips = out_ref.shape[0] // 4
    for quarter, block in enumerate(by_quarter(kept_ref, handed_ref, 0, chips)):
        out_ref[quarter * chips : (quarter + 1) * chips, :] = block


def merge_kernel(kept_ref, handed_ref, pieces_ref, out_ref):
    chips = out_ref.shape[0] // 5
    for quarter, block in enumerate(by_quarter(kept_ref, handed_ref, 2 * chips, chips)):
        out_ref[pl.ds(quarter, chips, stride=5), :] = block
    total = pieces_ref[:chips, :]
    for member in range(1, 4):
        total = total + pieces_ref[member * chips : (member + 1) * chips, :]
    out_ref[pl.ds(4, chips, stride=5), :] = total


def last_kernel(returned_ref, skipped_ref, input_ref, filter_ref):
    chips = returned_ref.shape[0] // 5
    filter_ref[...] = returned_ref[pl.ds(4, chips, stride=5), :]
    rows = [returned_ref[pl.ds(quarter, chips, stride=5), :] for quarter in range(4)]
    total = jnp.concatenate(rows, axis=0).T + skipped_ref[...]
    input_ref[...] = total.astype(jnp.bfloat16)


def exchange(values, axis):
    rows, columns = values.shape
    members = lax.axis_size(axis)
    wide = values.reshape(members, 1, rows // members * columns)
    wide = lax.all_to_all(wide, axis, split_axis=0, concat_axis=0, tiled=True)
    return wide.reshape(rows, columns)


def near(values):
    return pltpu.with_memory_space_constraint(values, pltpu.VMEM)


def local(inputs, out_grad, out_gate, filter_param, skip_gain):
    members = lax.axis_size(("chip", "core"))
    stride, channels = filter_param.shape
    f32 = jnp.float32
    packed, skipped = pl.pallas_call(
        pack_kernel,
        out_shape=[pltpu.VMEM((members * 6, stride), f32), pltpu.VMEM((stride, channels), f32)],
    )(inputs[0], out_grad[0], out_gate[0], filter_param, skip_gain[None, :])
    spread = exchange(packed, ("chip", "core"))
    constants = [near(jnp.asarray(table)) for table in tables(members, stride)]
    kept, handed = pl.pallas_call(
        spectra_kernel, out_shape=[pltpu.VMEM((members * 2, stride), f32)] * 2
    )(near(spread), *constants)
    handed = near(lax.ppermute(handed, "core", [(0, 1), (1, 0)]))
    kept = near(kept)
    slots = pl.pallas_call(slots_kernel, out_shape=pltpu.VMEM((members * 2, stride), f32))(
        kept, handed
    )
    pieces = exchange(slots, "rep")
    merged = pl.pallas_call(
        merge_kernel, out_shape=pltpu.VMEM((members // 2 * 5, stride), f32)
    )(kept, handed, near(pieces))
    returned = exchange(merged, "chip")
    input_part, filter_part = pl.pallas_call(
        last_kernel,
        out_shape=[
            jax.ShapeDtypeStruct((stride, channels), jnp.bfloat16),
            jax.ShapeDtypeStruct((channels // 4, stride), f32),
        ],
    )(near(returned), near(skipped))
    return (input_part[None], filter_part.T)


def solution(mesh):
    seqs, members = mesh.devices.shape
    cores = Mesh(mesh.devices.reshape(seqs, members // 2, 2), ("rep", "chip", "core"))
    ctx = ("chip", "core")
    return jax.shard_map(
        local,
        mesh=cores,
        in_specs=(
            P("rep", ctx, None),
            P("rep", ctx, None),
            P("rep", ctx, None),
            P(ctx, None),
            P(),
        ),
        out_specs=(P("rep", ctx, None), P(ctx, "rep")),
        check_vma=False,
    )
```

```python
import functools
import math

import jax
import jax.numpy as jnp
import numpy as np
from jax import lax
from jax.experimental import pallas as pl
from jax.experimental.pallas import tpu as pltpu
from jax.sharding import Mesh
from jax.sharding import PartitionSpec as P


def halves(values):
    high = values.astype(jnp.bfloat16)
    return high, (values - high.astype(jnp.float32)).astype(jnp.bfloat16)


def product(left, right):
    def dot(one, other):
        return jnp.dot(one, other, preferred_element_type=jnp.float32)

    total = dot(left[0], right[0])
    if right[1] is not None:
        total = total + dot(left[0], right[1])
    return total + dot(left[1], right[0])


def tables(members, stride):
    padded = 2 * members * stride
    t1 = np.arange(members)
    t2 = np.arange(stride)
    odd = 2 * np.arange(members) + 1
    outer = 2.0 * np.pi / (4 * members) * (odd[:, None] * t1[None, :] % (4 * members))
    twist = 2.0 * np.pi / (2 * padded) * (odd[:, None] * t2[None, :] % (2 * padded))
    inner = 2.0 * np.pi / stride * (t2[:, None] * t2[None, :] % stride)
    first = np.concatenate([np.cos(outer), -np.sin(outer)], axis=0)
    second = np.block([[np.cos(inner), -np.sin(inner)], [np.sin(inner), np.cos(inner)]])
    scale = 2.0 / padded / math.sqrt(members * stride)
    result = [np.asarray(np.cos(twist), np.float32), np.asarray(np.sin(twist), np.float32)]
    last = np.concatenate([first.T[0::2], first.T[1::2]], axis=0) * scale
    for table in (first, second, second.T, last):
        high = table.astype(jnp.bfloat16)
        result += [high, (table - high.astype(np.float64)).astype(jnp.bfloat16)]
    return result


def pack_kernel(inputs_ref, grad_ref, gate_ref, filter_ref, skip_ref, out_ref, skipped_ref):
    gated = grad_ref[...].astype(jnp.float32) * gate_ref[...].astype(jnp.float32)
    skipped_ref[...] = gated * skip_ref[...]
    signals = (gated, inputs_ref[...].astype(jnp.float32), filter_ref[...])
    chips = out_ref.shape[0] // 12
    for index, signal in enumerate(signals):
        turned = signal.T
        for quarter in range(4):
            row = 6 * (quarter // 2) + 2 * index + quarter % 2
            out_ref[pl.ds(row, chips, stride=12), :] = turned[
                quarter * chips : (quarter + 1) * chips
            ]


def spectra(signal_ref, first, second, cosine, sine):
    stride = signal_ref.shape[1]
    members = signal_ref.shape[0] // 6
    signals = [signal_ref[pl.ds(row, members, stride=6), :] for row in range(6)]
    partial = []
    for row in range(0, 6, 2):
        pair = jnp.concatenate(signals[row : row + 2], axis=1)
        sides = (pair.astype(jnp.bfloat16), None) if row == 2 else halves(pair)
        both = product(first, sides)
        partial += [both[:, :stride], both[:, stride:]]
    parts = []
    for value in partial:
        real, imag = value[:members], value[members:]
        turned = jnp.concatenate(
            [real * cosine + imag * sine, imag * cosine - real * sine], axis=1
        )
        parts.append(product(halves(turned), second))
    return parts


def correlated(one, other):
    stride = one.shape[1] // 2
    real, imag = one[:, :stride], one[:, stride:]
    other_real, other_imag = other[:, :stride], other[:, stride:]
    return jnp.concatenate(
        [real * other_real + imag * other_imag, imag * other_real - real * other_imag], axis=1
    )


def inverse(values, back, last, cosine, sine):
    columns = []
    for value in values:
        restored = product(halves(value), back)
        stride = restored.shape[1] // 2
        real, imag = restored[:, :stride], restored[:, stride:]
        columns.append(
            jnp.concatenate([real * cosine - imag * sine, imag * cosine + real * sine], axis=0)
        )
    return product(last, halves(jnp.concatenate(columns, axis=1)))


def pairs_of(refs):
    return [(refs[at][...], refs[at + 1][...]) for at in range(0, len(refs), 2)]


def spectra_kernel(signal_ref, cos_ref, sin_ref, *refs):
    first, second, back, last = pairs_of(refs[:8])
    kept_ref, handed_ref = refs[8:]
    stride = signal_ref.shape[1]
    chips = signal_ref.shape[0] // 12
    even_core = lax.axis_index("core") == 0
    cosine, sine = cos_ref[...], sin_ref[...]
    parts = spectra(signal_ref, first, second, cosine, sine)
    last = [
        jnp.where(even_core, half, jnp.concatenate([half[chips:], half[:chips]], axis=0))
        for half in last
    ]
    for index, other in enumerate((2, 4)):
        products = [correlated(parts[part], parts[other + part]) for part in range(2)]
        values = inverse(products, back, last, cosine, sine)
        for part in range(2):
            columns = slice(part * stride, (part + 1) * stride)
            rows = slice((2 * index + part) * chips, (2 * index + part + 1) * chips)
            kept_ref[rows, :] = values[:chips, columns]
            handed_ref[rows, :] = values[chips:, columns]


def by_quarter(kept_ref, handed_ref, row, chips):
    even_core = lax.axis_index("core") == 0
    first, second = [], []
    for part in range(2):
        rows = slice(row + part * chips, row + (part + 1) * chips)
        mine, other = kept_ref[rows, :], handed_ref[rows, :]
        first.append(jnp.where(even_core, mine, other))
        second.append(jnp.where(even_core, other, mine))
    return first + second


def slots_kernel(kept_ref, handed_ref, out_ref):
    chips = out_ref.shape[0] // 4
    for quarter, block in enumerate(by_quarter(kept_ref, handed_ref, 0, chips)):
        out_ref[quarter * chips : (quarter + 1) * chips, :] = block


def merge_kernel(kept_ref, handed_ref, pieces_ref, out_ref):
    chips = out_ref.shape[0] // 5
    for quarter, block in enumerate(by_quarter(kept_ref, handed_ref, 2 * chips, chips)):
        out_ref[pl.ds(quarter, chips, stride=5), :] = block
    total = pieces_ref[:chips, :]
    for member in range(1, 4):
        total = total + pieces_ref[member * chips : (member + 1) * chips, :]
    out_ref[pl.ds(4, chips, stride=5), :] = total


def last_kernel(returned_ref, skipped_ref, input_ref, filter_ref):
    chips = returned_ref.shape[0] // 5
    filter_ref[...] = returned_ref[pl.ds(4, chips, stride=5), :]
    rows = [returned_ref[pl.ds(quarter, chips, stride=5), :] for quarter in range(4)]
    total = jnp.concatenate(rows, axis=0).T + skipped_ref[...]
    input_ref[...] = total.astype(jnp.bfloat16)


def exchange(values, axis):
    rows, columns = values.shape
    members = lax.axis_size(axis)
    wide = values.reshape(members, 1, rows // members * columns)
    wide = lax.all_to_all(wide, axis, split_axis=0, concat_axis=0, tiled=True)
    return wide.reshape(rows, columns)


def near(values):
    return pltpu.with_memory_space_constraint(values, pltpu.VMEM)


def local(inputs, out_grad, out_gate, filter_param, skip_gain):
    members = lax.axis_size(("chip", "core"))
    stride, channels = filter_param.shape
    f32 = jnp.float32
    packed, skipped = pl.pallas_call(
        pack_kernel,
        out_shape=[pltpu.VMEM((members * 6, stride), f32), pltpu.VMEM((stride, channels), f32)],
    )(inputs[0], out_grad[0], out_gate[0], filter_param, skip_gain[None, :])
    spread = exchange(packed, ("chip", "core"))
    constants = [near(jnp.asarray(table)) for table in tables(members, stride)]
    kept, handed = pl.pallas_call(
        spectra_kernel, out_shape=[pltpu.VMEM((members * 2, stride), f32)] * 2
    )(near(spread), *constants)
    handed = near(lax.ppermute(handed, "core", [(0, 1), (1, 0)]))
    kept = near(kept)
    slots = pl.pallas_call(slots_kernel, out_shape=pltpu.VMEM((members * 2, stride), f32))(
        kept, handed
    )
    pieces = exchange(slots, "rep")
    merged = pl.pallas_call(
        merge_kernel, out_shape=pltpu.VMEM((members // 2 * 5, stride), f32)
    )(kept, handed, near(pieces))
    returned = exchange(merged, "chip")
    input_part, filter_part = pl.pallas_call(
        last_kernel,
        out_shape=[
            jax.ShapeDtypeStruct((stride, channels), jnp.bfloat16),
            jax.ShapeDtypeStruct((channels // 4, stride), f32),
        ],
    )(near(returned), near(skipped))
    return (input_part[None], filter_part.T)


def solution(mesh):
    seqs, members = mesh.devices.shape
    cores = Mesh(mesh.devices.reshape(seqs, members // 2, 2), ("rep", "chip", "core"))
    ctx = ("chip", "core")
    return jax.shard_map(
        local,
        mesh=cores,
        in_specs=(
            P("rep", ctx, None),
            P("rep", ctx, None),
            P("rep", ctx, None),
            P(ctx, None),
            P(),
        ),
        out_specs=(P("rep", ctx, None), P(ctx, "rep")),
        check_vma=False,
    )
```

```python
import functools
import math

import jax
import jax.numpy as jnp
import numpy as np
from jax import lax
from jax.experimental import pallas as pl
from jax.experimental.pallas import tpu as pltpu
from jax.sharding import Mesh
from jax.sharding import PartitionSpec as P


def halves(values):
    high = values.astype(jnp.bfloat16)
    return high, (values - high.astype(jnp.float32)).astype(jnp.bfloat16)


def product(left, right):
    def dot(one, other):
        return jnp.dot(one, other, preferred_element_type=jnp.float32)

    total = dot(left[0], right[0])
    if right[1] is not None:
        total = total + dot(left[0], right[1])
    return total + dot(left[1], right[0])


def tables(members, stride):
    padded = 2 * members * stride
    t1 = np.arange(members)
    t2 = np.arange(stride)
    odd = 2 * np.arange(members) + 1
    outer = 2.0 * np.pi / (4 * members) * (odd[:, None] * t1[None, :] % (4 * members))
    twist = 2.0 * np.pi / (2 * padded) * (odd[:, None] * t2[None, :] % (2 * padded))
    inner = 2.0 * np.pi / stride * (t2[:, None] * t2[None, :] % stride)
    first = np.concatenate([np.cos(outer), -np.sin(outer)], axis=0)
    second = np.block([[np.cos(inner), -np.sin(inner)], [np.sin(inner), np.cos(inner)]])
    scale = 2.0 / padded / math.sqrt(members * stride)
    result = [np.asarray(np.cos(twist), np.float32), np.asarray(np.sin(twist), np.float32)]
    last = np.concatenate([first.T[0::2], first.T[1::2]], axis=0) * scale
    for table in (first, second, second.T, last):
        high = table.astype(jnp.bfloat16)
        result += [high, (table - high.astype(np.float64)).astype(jnp.bfloat16)]
    return result


def pack_kernel(inputs_ref, grad_ref, gate_ref, filter_ref, skip_ref, out_ref, skipped_ref):
    gated = grad_ref[...].astype(jnp.float32) * gate_ref[...].astype(jnp.float32)
    skipped_ref[...] = gated * skip_ref[...]
    signals = (gated, inputs_ref[...].astype(jnp.float32), filter_ref[...])
    chips = out_ref.shape[0] // 12
    for index, signal in enumerate(signals):
        turned = signal.T
        for quarter in range(4):
            row = 6 * (quarter // 2) + 2 * index + quarter % 2
            out_ref[pl.ds(row, chips, stride=12), :] = turned[
                quarter * chips : (quarter + 1) * chips
            ]


def spectra(signal_ref, first, second, cosine, sine):
    stride = signal_ref.shape[1]
    members = signal_ref.shape[0] // 6
    signals = [signal_ref[pl.ds(row, members, stride=6), :] for row in range(6)]
    partial = []
    for row in range(0, 6, 2):
        pair = jnp.concatenate(signals[row : row + 2], axis=1)
        sides = (pair.astype(jnp.bfloat16), None) if row == 2 else halves(pair)
        both = product(first, sides)
        partial += [both[:, :stride], both[:, stride:]]
    parts = []
    for value in partial:
        real, imag = value[:members], value[members:]
        turned = jnp.concatenate(
            [real * cosine + imag * sine, imag * cosine - real * sine], axis=1
        )
        parts.append(product(halves(turned), second))
    return parts


def correlated(one, other):
    stride = one.shape[1] // 2
    real, imag = one[:, :stride], one[:, stride:]
    other_real, other_imag = other[:, :stride], other[:, stride:]
    return jnp.concatenate(
        [real * other_real + imag * other_imag, imag * other_real - real * other_imag], axis=1
    )


def inverse(values, back, last, cosine, sine):
    columns = []
    for value in values:
        restored = product(halves(value), back)
        stride = restored.shape[1] // 2
        real, imag = restored[:, :stride], restored[:, stride:]
        columns.append(
            jnp.concatenate([real * cosine - imag * sine, imag * cosine + real * sine], axis=0)
        )
    return product(last, halves(jnp.concatenate(columns, axis=1)))


def pairs_of(refs):
    return [(refs[at][...], refs[at + 1][...]) for at in range(0, len(refs), 2)]


def spectra_kernel(signal_ref, cos_ref, sin_ref, *refs):
    first, second, back, last = pairs_of(refs[:8])
    kept_ref, handed_ref = refs[8:]
    stride = signal_ref.shape[1]
    chips = signal_ref.shape[0] // 12
    even_core = lax.axis_index("core") == 0
    cosine, sine = cos_ref[...], sin_ref[...]
    parts = spectra(signal_ref, first, second, cosine, sine)
    for index, other in enumerate((2, 4)):
        products = [correlated(parts[part], parts[other + part]) for part in range(2)]
        values = inverse(products, back, last, cosine, sine)
        for part in range(2):
            even = values[:chips, part * stride : (part + 1) * stride]
            odd = values[chips:, part * stride : (part + 1) * stride]
            rows = slice((2 * index + part) * chips, (2 * index + part + 1) * chips)
            kept_ref[rows, :] = jnp.where(even_core, even, odd)
            handed_ref[rows, :] = jnp.where(even_core, odd, even)


def by_quarter(kept_ref, handed_ref, row, chips):
    even_core = lax.axis_index("core") == 0
    first, second = [], []
    for part in range(2):
        rows = slice(row + part * chips, row + (part + 1) * chips)
        mine, other = kept_ref[rows, :], handed_ref[rows, :]
        first.append(jnp.where(even_core, mine, other))
        second.append(jnp.where(even_core, other, mine))
    return first + second


def slots_kernel(kept_ref, handed_ref, out_ref):
    chips = out_ref.shape[0] // 4
    for quarter, block in enumerate(by_quarter(kept_ref, handed_ref, 0, chips)):
        out_ref[quarter * chips : (quarter + 1) * chips, :] = block


def merge_kernel(kept_ref, handed_ref, pieces_ref, out_ref):
    chips = out_ref.shape[0] // 5
    for quarter, block in enumerate(by_quarter(kept_ref, handed_ref, 2 * chips, chips)):
        out_ref[pl.ds(quarter, chips, stride=5), :] = block
    total = pieces_ref[:chips, :]
    for member in range(1, 4):
        total = total + pieces_ref[member * chips : (member + 1) * chips, :]
    out_ref[pl.ds(4, chips, stride=5), :] = total


def last_kernel(returned_ref, skipped_ref, input_ref, filter_ref):
    chips = returned_ref.shape[0] // 5
    filter_ref[...] = returned_ref[pl.ds(4, chips, stride=5), :]
    rows = [returned_ref[pl.ds(quarter, chips, stride=5), :] for quarter in range(4)]
    total = jnp.concatenate(rows, axis=0).T + skipped_ref[...]
    input_ref[...] = total.astype(jnp.bfloat16)


def exchange(values, axis):
    rows, columns = values.shape
    members = lax.axis_size(axis)
    wide = values.reshape(members, 1, rows // members * columns)
    wide = lax.all_to_all(wide, axis, split_axis=0, concat_axis=0, tiled=True)
    return wide.reshape(rows, columns)


def near(values):
    return pltpu.with_memory_space_constraint(values, pltpu.VMEM)


def local(inputs, out_grad, out_gate, filter_param, skip_gain):
    members = lax.axis_size(("chip", "core"))
    stride, channels = filter_param.shape
    f32 = jnp.float32
    packed, skipped = pl.pallas_call(
        pack_kernel,
        out_shape=[pltpu.VMEM((members * 6, stride), f32), pltpu.VMEM((stride, channels), f32)],
    )(inputs[0], out_grad[0], out_gate[0], filter_param, skip_gain[None, :])
    spread = exchange(packed, ("chip", "core"))
    constants = [near(jnp.asarray(table)) for table in tables(members, stride)]
    kept, handed = pl.pallas_call(
        spectra_kernel, out_shape=[pltpu.VMEM((members * 2, stride), f32)] * 2
    )(near(spread), *constants)
    handed = near(lax.ppermute(handed, "core", [(0, 1), (1, 0)]))
    kept = near(kept)
    slots = pl.pallas_call(slots_kernel, out_shape=pltpu.VMEM((members * 2, stride), f32))(
        kept, handed
    )
    pieces = lax.all_to_all(slots, "rep", split_axis=0, concat_axis=0, tiled=True)
    merged = pl.pallas_call(
        merge_kernel, out_shape=pltpu.VMEM((members // 2 * 5, stride), f32)
    )(kept, handed, near(pieces))
    returned = exchange(merged, "chip")
    input_part, filter_part = pl.pallas_call(
        last_kernel,
        out_shape=[
            jax.ShapeDtypeStruct((stride, channels), jnp.bfloat16),
            jax.ShapeDtypeStruct((channels // 4, stride), f32),
        ],
    )(near(returned), near(skipped))
    return (input_part[None], filter_part.T)


def solution(mesh):
    seqs, members = mesh.devices.shape
    cores = Mesh(mesh.devices.reshape(seqs, members // 2, 2), ("rep", "chip", "core"))
    ctx = ("chip", "core")
    return jax.shard_map(
        local,
        mesh=cores,
        in_specs=(
            P("rep", ctx, None),
            P("rep", ctx, None),
            P("rep", ctx, None),
            P(ctx, None),
            P(),
        ),
        out_specs=(P("rep", ctx, None), P(ctx, "rep")),
        check_vma=False,
    )
```

```python
import functools
import math

import jax
import jax.numpy as jnp
import numpy as np
from jax import lax
from jax.experimental import pallas as pl
from jax.experimental.pallas import tpu as pltpu
from jax.sharding import Mesh
from jax.sharding import PartitionSpec as P


def halves(values):
    high = values.astype(jnp.bfloat16)
    return high, (values - high.astype(jnp.float32)).astype(jnp.bfloat16)


def product(left, right):
    def dot(one, other):
        return jnp.dot(one, other, preferred_element_type=jnp.float32)

    total = dot(left[0], right[0])
    if right[1] is not None:
        total = total + dot(left[0], right[1])
    return total + dot(left[1], right[0])


def tables(members, stride):
    padded = 2 * members * stride
    t1 = np.arange(members)
    t2 = np.arange(stride)
    odd = 2 * np.arange(members) + 1
    outer = 2.0 * np.pi / (4 * members) * (odd[:, None] * t1[None, :] % (4 * members))
    twist = 2.0 * np.pi / (2 * padded) * (odd[:, None] * t2[None, :] % (2 * padded))
    inner = 2.0 * np.pi / stride * (t2[:, None] * t2[None, :] % stride)
    first = np.concatenate([np.cos(outer), -np.sin(outer)], axis=0)
    second = np.block([[np.cos(inner), -np.sin(inner)], [np.sin(inner), np.cos(inner)]])
    scale = 2.0 / padded / math.sqrt(members * stride)
    result = [np.concatenate([np.cos(twist), np.sin(twist)], axis=0).astype(np.float32)]
    last = np.concatenate([first.T[0::2], first.T[1::2]], axis=0) * scale
    for table in (first, second, second.T, last):
        high = table.astype(jnp.bfloat16)
        low = (table - high.astype(np.float64)).astype(jnp.bfloat16)
        result.append(np.concatenate([high, low], axis=0))
    return result


def pack_kernel(inputs_ref, grad_ref, gate_ref, filter_ref, skip_ref, out_ref, skipped_ref):
    gated = grad_ref[...].astype(jnp.float32) * gate_ref[...].astype(jnp.float32)
    skipped_ref[...] = gated * skip_ref[...]
    signals = (gated, inputs_ref[...].astype(jnp.float32), filter_ref[...])
    chips = out_ref.shape[0] // 12
    for index, signal in enumerate(signals):
        turned = signal.T
        for quarter in range(4):
            row = 6 * (quarter // 2) + 2 * index + quarter % 2
            out_ref[pl.ds(row, chips, stride=12), :] = turned[
                quarter * chips : (quarter + 1) * chips
            ]


def spectra(signal_ref, first, second, cosine, sine):
    stride = signal_ref.shape[1]
    members = signal_ref.shape[0] // 6
    signals = [signal_ref[pl.ds(row, members, stride=6), :] for row in range(6)]
    partial = []
    for row in range(0, 6, 2):
        pair = jnp.concatenate(signals[row : row + 2], axis=1)
        sides = (pair.astype(jnp.bfloat16), None) if row == 2 else halves(pair)
        both = product(first, sides)
        partial += [both[:, :stride], both[:, stride:]]
    parts = []
    for value in partial:
        real, imag = value[:members], value[members:]
        turned = jnp.concatenate(
            [real * cosine + imag * sine, imag * cosine - real * sine], axis=1
        )
        parts.append(product(halves(turned), second))
    return parts


def correlated(one, other):
    stride = one.shape[1] // 2
    real, imag = one[:, :stride], one[:, stride:]
    other_real, other_imag = other[:, :stride], other[:, stride:]
    return jnp.concatenate(
        [real * other_real + imag * other_imag, imag * other_real - real * other_imag], axis=1
    )


def inverse(values, back, last, cosine, sine):
    columns = []
    for value in values:
        restored = product(halves(value), back)
        stride = restored.shape[1] // 2
        real, imag = restored[:, :stride], restored[:, stride:]
        columns.append(
            jnp.concatenate([real * cosine - imag * sine, imag * cosine + real * sine], axis=0)
        )
    return product(last, halves(jnp.concatenate(columns, axis=1)))


def pair_of(ref):
    rows = ref.shape[0] // 2
    return ref[:rows, :], ref[rows:, :]


def spectra_kernel(signal_ref, twist_ref, *refs):
    first, second, back, last = [pair_of(ref) for ref in refs[:4]]
    kept_ref, handed_ref = refs[4:]
    stride = signal_ref.shape[1]
    chips = signal_ref.shape[0] // 12
    even_core = lax.axis_index("core") == 0
    cosine, sine = pair_of(twist_ref)
    parts = spectra(signal_ref, first, second, cosine, sine)
    for index, other in enumerate((2, 4)):
        products = [correlated(parts[part], parts[other + part]) for part in range(2)]
        values = inverse(products, back, last, cosine, sine)
        for part in range(2):
            even = values[:chips, part * stride : (part + 1) * stride]
            odd = values[chips:, part * stride : (part + 1) * stride]
            rows = slice((2 * index + part) * chips, (2 * index + part + 1) * chips)
            kept_ref[rows, :] = jnp.where(even_core, even, odd)
            handed_ref[rows, :] = jnp.where(even_core, odd, even)


def by_quarter(kept_ref, handed_ref, row, chips):
    even_core = lax.axis_index("core") == 0
    first, second = [], []
    for part in range(2):
        rows = slice(row + part * chips, row + (part + 1) * chips)
        mine, other = kept_ref[rows, :], handed_ref[rows, :]
        first.append(jnp.where(even_core, mine, other))
        second.append(jnp.where(even_core, other, mine))
    return first + second


def slots_kernel(kept_ref, handed_ref, out_ref):
    chips = out_ref.shape[0] // 4
    for quarter, block in enumerate(by_quarter(kept_ref, handed_ref, 0, chips)):
        out_ref[quarter * chips : (quarter + 1) * chips, :] = block


def merge_kernel(kept_ref, handed_ref, pieces_ref, out_ref):
    chips = out_ref.shape[0] // 5
    for quarter, block in enumerate(by_quarter(kept_ref, handed_ref, 2 * chips, chips)):
        out_ref[pl.ds(quarter, chips, stride=5), :] = block
    total = pieces_ref[:chips, :]
    for member in range(1, 4):
        total = total + pieces_ref[member * chips : (member + 1) * chips, :]
    out_ref[pl.ds(4, chips, stride=5), :] = total


def last_kernel(returned_ref, skipped_ref, input_ref, filter_ref):
    chips = returned_ref.shape[0] // 5
    filter_ref[...] = returned_ref[pl.ds(4, chips, stride=5), :]
    rows = [returned_ref[pl.ds(quarter, chips, stride=5), :] for quarter in range(4)]
    total = jnp.concatenate(rows, axis=0).T + skipped_ref[...]
    input_ref[...] = total.astype(jnp.bfloat16)


def exchange(values, axis):
    rows, columns = values.shape
    members = lax.axis_size(axis)
    wide = values.reshape(members, 1, rows // members * columns)
    wide = lax.all_to_all(wide, axis, split_axis=0, concat_axis=0, tiled=True)
    return wide.reshape(rows, columns)


def near(values):
    return pltpu.with_memory_space_constraint(values, pltpu.VMEM)


def local(inputs, out_grad, out_gate, filter_param, skip_gain):
    members = lax.axis_size(("chip", "core"))
    stride, channels = filter_param.shape
    f32 = jnp.float32
    packed, skipped = pl.pallas_call(
        pack_kernel,
        out_shape=[pltpu.VMEM((members * 6, stride), f32), pltpu.VMEM((stride, channels), f32)],
    )(inputs[0], out_grad[0], out_gate[0], filter_param, skip_gain[None, :])
    spread = exchange(packed, ("chip", "core"))
    constants = [near(jnp.asarray(table)) for table in tables(members, stride)]
    kept, handed = pl.pallas_call(
        spectra_kernel, out_shape=[pltpu.VMEM((members * 2, stride), f32)] * 2
    )(near(spread), *constants)
    handed = near(lax.ppermute(handed, "core", [(0, 1), (1, 0)]))
    kept = near(kept)
    slots = pl.pallas_call(slots_kernel, out_shape=pltpu.VMEM((members * 2, stride), f32))(
        kept, handed
    )
    pieces = exchange(slots, "rep")
    merged = pl.pallas_call(
        merge_kernel, out_shape=pltpu.VMEM((members // 2 * 5, stride), f32)
    )(kept, handed, near(pieces))
    returned = exchange(merged, "chip")
    input_part, filter_part = pl.pallas_call(
        last_kernel,
        out_shape=[
            jax.ShapeDtypeStruct((stride, channels), jnp.bfloat16),
            jax.ShapeDtypeStruct((channels // 4, stride), f32),
        ],
    )(near(returned), near(skipped))
    return (input_part[None], filter_part.T)


def solution(mesh):
    seqs, members = mesh.devices.shape
    cores = Mesh(mesh.devices.reshape(seqs, members // 2, 2), ("rep", "chip", "core"))
    ctx = ("chip", "core")
    return jax.shard_map(
        local,
        mesh=cores,
        in_specs=(
            P("rep", ctx, None),
            P("rep", ctx, None),
            P("rep", ctx, None),
            P(ctx, None),
            P(),
        ),
        out_specs=(P("rep", ctx, None), P(ctx, "rep")),
        check_vma=False,
    )
```

```python
import functools
import math

import jax
import jax.numpy as jnp
import numpy as np
from jax import lax
from jax.experimental import pallas as pl
from jax.experimental.pallas import tpu as pltpu
from jax.sharding import Mesh
from jax.sharding import PartitionSpec as P


def halves(values):
    high = values.astype(jnp.bfloat16)
    return high, (values - high.astype(jnp.float32)).astype(jnp.bfloat16)


def product(left, right):
    def dot(one, other):
        return jnp.dot(one, other, preferred_element_type=jnp.float32)

    total = dot(left[0], right[0])
    if right[1] is not None:
        total = total + dot(left[0], right[1])
    return total + dot(left[1], right[0])


def tables(members, stride):
    padded = 2 * members * stride
    t1 = np.arange(members)
    t2 = np.arange(stride)
    odd = 2 * np.arange(members) + 1
    outer = 2.0 * np.pi / (4 * members) * (odd[:, None] * t1[None, :] % (4 * members))
    twist = 2.0 * np.pi / (2 * padded) * (odd[:, None] * t2[None, :] % (2 * padded))
    inner = 2.0 * np.pi / stride * (t2[:, None] * t2[None, :] % stride)
    first = np.concatenate([np.cos(outer), -np.sin(outer)], axis=0)
    second = np.block([[np.cos(inner), -np.sin(inner)], [np.sin(inner), np.cos(inner)]])
    scale = 2.0 / padded / math.sqrt(members * stride)
    result = [np.concatenate([np.cos(twist), np.sin(twist)], axis=0).astype(np.float32)]
    last = np.concatenate([first.T[0::2], first.T[1::2]], axis=0) * scale
    for table in (first, second, second.T, last):
        high = table.astype(jnp.bfloat16)
        low = (table - high.astype(np.float64)).astype(jnp.bfloat16)
        result.append(np.concatenate([high, low], axis=0))
    return result


def pack_kernel(inputs_ref, grad_ref, gate_ref, filter_ref, skip_ref, out_ref, skipped_ref):
    gated = grad_ref[...].astype(jnp.float32) * gate_ref[...].astype(jnp.float32)
    skipped_ref[...] = gated * skip_ref[...]
    signals = (gated, inputs_ref[...].astype(jnp.float32), filter_ref[...])
    chips = out_ref.shape[0] // 12
    for index, signal in enumerate(signals):
        turned = signal.T
        for quarter in range(4):
            row = 6 * (quarter // 2) + 2 * index + quarter % 2
            out_ref[pl.ds(row, chips, stride=12), :] = turned[
                quarter * chips : (quarter + 1) * chips
            ]


def spectra(signal_ref, first, second, cosine, sine):
    stride = signal_ref.shape[1]
    members = signal_ref.shape[0] // 6
    signals = [signal_ref[pl.ds(row, members, stride=6), :] for row in range(6)]
    partial = []
    for row in range(0, 6, 2):
        pair = jnp.concatenate(signals[row : row + 2], axis=1)
        sides = (pair.astype(jnp.bfloat16), None) if row == 2 else halves(pair)
        both = product(first, sides)
        partial += [both[:, :stride], both[:, stride:]]
    parts = []
    for value in partial:
        real, imag = value[:members], value[members:]
        turned = jnp.concatenate(
            [real * cosine + imag * sine, imag * cosine - real * sine], axis=1
        )
        parts.append(product(halves(turned), second))
    return parts


def correlated(one, other):
    stride = one.shape[1] // 2
    real, imag = one[:, :stride], one[:, stride:]
    other_real, other_imag = other[:, :stride], other[:, stride:]
    return jnp.concatenate(
        [real * other_real + imag * other_imag, imag * other_real - real * other_imag], axis=1
    )


def inverse(values, back, last, cosine, sine):
    columns = []
    for value in values:
        restored = product(halves(value), back)
        stride = restored.shape[1] // 2
        real, imag = restored[:, :stride], restored[:, stride:]
        columns.append(
            jnp.concatenate([real * cosine - imag * sine, imag * cosine + real * sine], axis=0)
        )
    return product(last, halves(jnp.concatenate(columns, axis=1)))


def pair_of(ref):
    rows = ref.shape[0] // 2
    return ref[:rows, :], ref[rows:, :]


def spectra_kernel(signal_ref, twist_ref, *refs):
    first, second, back, last = [pair_of(ref) for ref in refs[:4]]
    kept_ref, handed_ref = refs[4:]
    stride = signal_ref.shape[1]
    chips = signal_ref.shape[0] // 12
    even_core = lax.axis_index("core") == 0
    cosine, sine = pair_of(twist_ref)
    parts = spectra(signal_ref, first, second, cosine, sine)
    last = [
        jnp.where(even_core, half, jnp.concatenate([half[chips:], half[:chips]], axis=0))
        for half in last
    ]
    for index, other in enumerate((2, 4)):
        products = [correlated(parts[part], parts[other + part]) for part in range(2)]
        values = inverse(products, back, last, cosine, sine)
        for part in range(2):
            columns = slice(part * stride, (part + 1) * stride)
            rows = slice((2 * index + part) * chips, (2 * index + part + 1) * chips)
            kept_ref[rows, :] = values[:chips, columns]
            handed_ref[rows, :] = values[chips:, columns]


def by_quarter(kept_ref, handed_ref, row, chips):
    even_core = lax.axis_index("core") == 0
    first, second = [], []
    for part in range(2):
        rows = slice(row + part * chips, row + (part + 1) * chips)
        mine, other = kept_ref[rows, :], handed_ref[rows, :]
        first.append(jnp.where(even_core, mine, other))
        second.append(jnp.where(even_core, other, mine))
    return first + second


def slots_kernel(kept_ref, handed_ref, out_ref):
    chips = out_ref.shape[0] // 4
    for quarter, block in enumerate(by_quarter(kept_ref, handed_ref, 0, chips)):
        out_ref[quarter * chips : (quarter + 1) * chips, :] = block


def merge_kernel(kept_ref, handed_ref, pieces_ref, out_ref):
    chips = out_ref.shape[0] // 5
    for quarter, block in enumerate(by_quarter(kept_ref, handed_ref, 2 * chips, chips)):
        out_ref[pl.ds(quarter, chips, stride=5), :] = block
    total = pieces_ref[:chips, :]
    for member in range(1, 4):
        total = total + pieces_ref[member * chips : (member + 1) * chips, :]
    out_ref[pl.ds(4, chips, stride=5), :] = total


def last_kernel(returned_ref, skipped_ref, input_ref, filter_ref):
    chips = returned_ref.shape[0] // 5
    filter_ref[...] = returned_ref[pl.ds(4, chips, stride=5), :]
    rows = [returned_ref[pl.ds(quarter, chips, stride=5), :] for quarter in range(4)]
    total = jnp.concatenate(rows, axis=0).T + skipped_ref[...]
    input_ref[...] = total.astype(jnp.bfloat16)


def exchange(values, axis):
    rows, columns = values.shape
    members = lax.axis_size(axis)
    wide = values.reshape(members, 1, rows // members * columns)
    wide = lax.all_to_all(wide, axis, split_axis=0, concat_axis=0, tiled=True)
    return wide.reshape(rows, columns)


def near(values):
    return pltpu.with_memory_space_constraint(values, pltpu.VMEM)


def local(inputs, out_grad, out_gate, filter_param, skip_gain):
    members = lax.axis_size(("chip", "core"))
    stride, channels = filter_param.shape
    f32 = jnp.float32
    packed, skipped = pl.pallas_call(
        pack_kernel,
        out_shape=[pltpu.VMEM((members * 6, stride), f32), pltpu.VMEM((stride, channels), f32)],
    )(inputs[0], out_grad[0], out_gate[0], filter_param, skip_gain[None, :])
    spread = exchange(packed, ("chip", "core"))
    constants = [near(jnp.asarray(table)) for table in tables(members, stride)]
    kept, handed = pl.pallas_call(
        spectra_kernel, out_shape=[pltpu.VMEM((members * 2, stride), f32)] * 2
    )(near(spread), *constants)
    handed = near(lax.ppermute(handed, "core", [(0, 1), (1, 0)]))
    kept = near(kept)
    slots = pl.pallas_call(slots_kernel, out_shape=pltpu.VMEM((members * 2, stride), f32))(
        kept, handed
    )
    pieces = exchange(slots, "rep")
    merged = pl.pallas_call(
        merge_kernel, out_shape=pltpu.VMEM((members // 2 * 5, stride), f32)
    )(kept, handed, near(pieces))
    returned = exchange(merged, "chip")
    input_part, filter_part = pl.pallas_call(
        last_kernel,
        out_shape=[
            jax.ShapeDtypeStruct((stride, channels), jnp.bfloat16),
            jax.ShapeDtypeStruct((channels // 4, stride), f32),
        ],
    )(near(returned), near(skipped))
    return (input_part[None], filter_part.T)


def solution(mesh):
    seqs, members = mesh.devices.shape
    cores = Mesh(mesh.devices.reshape(seqs, members // 2, 2), ("rep", "chip", "core"))
    ctx = ("chip", "core")
    return jax.shard_map(
        local,
        mesh=cores,
        in_specs=(
            P("rep", ctx, None),
            P("rep", ctx, None),
            P("rep", ctx, None),
            P(ctx, None),
            P(),
        ),
        out_specs=(P("rep", ctx, None), P(ctx, "rep")),
        check_vma=False,
    )
```
